32 devices in a mesh: grp: 8 (over z, x), rot: 4 (over y, core).
Axes of the slice: x: 2, y: 2, z: 4, core: 2. Of those that a mesh axis runs over, the one named last changes fastest.
Arguments:
- features: bfloat16 [32768, 256], P(('grp', 'rot')), may hold values from -64 to 64
- w_msg: bfloat16 [2, 256, 256], replicated, may hold values from -0.375 to 0.375
- w_upd: bfloat16 [2, 256, 256], replicated, may hold values from -0.375 to 0.375
- local_tiles: bfloat16 [8, 4, 8, 3, 128, 128], P('grp', 'rot'), may hold values from -0.25 to 0.25
- local_src: int32 [8, 4, 8, 3], P('grp', 'rot'), may hold values from 0 to 7
- local_live: int32 [8, 4, 8, 3], P('grp', 'rot'), may hold values 0 or 1
- border_tiles: bfloat16 [8, 4, 4, 128, 128], P('grp', 'rot'), may hold values from -0.25 to 0.25
- border_rows: int32 [8, 4, 4, 128], P('grp', 'rot'), may hold values from 0 to 1023
- border_block: int32 [8, 4, 4], P('grp', 'rot'), may hold values from 0 to 7
- ball_order: int32 [8, 4, 1024], P('grp', 'rot'), may hold values from 0 to 1023, each once within a row
- w_ball_qkv: bfloat16 [256, 768], replicated, may hold values from -32 to 32
- w_ball_out: bfloat16 [256, 256], replicated, may hold values from -0.375 to 0.375
- w_mlp_in: bfloat16 [256, 1024], replicated, may hold values from -0.375 to 0.375
- w_mlp_out: bfloat16 [1024, 256], replicated, may hold values from -0.1875 to 0.1875
- w_rot_qkv: bfloat16 [256, 768], replicated, may hold values from -32 to 32
- w_rot_out: bfloat16 [256, 256], replicated, may hold values from -0.375 to 0.375
- relay_peer: int32 [8, 4, 1024], P('grp', 'rot'), may hold values from 0 to 3, as said below
- relay_rank: int32 [8, 4, 1024], P('grp', 'rot'), may hold values from 0 to 511, as said below
- relay_inbox: int32 [8, 4, 4, 512], P('grp', 'rot'), may hold values from 0 to 1024, as said below
Outputs:
- points_out: float32 [32768, 256], P(('grp', 'rot'))
The draws below stay inside these ranges and needn't reach their ends.
Inputs may be any that keep to these rules, and one draw needn't show every extreme that they name: `relay_peer`: each partition (g, r) relays exactly 512 of its points to partition (g, (r + 1) mod 4) and at most 171 to each other partition of its group, itself included, with 171 reached; every partition owns exactly 1024 points. `relay_rank`: for a fixed partition and owner, the ranks of the relayed points are 0, 1, 2 and so on without gaps. relay_inbox[g, o, s, c] is the owner row of the point that (g, s) relays to (g, o) with rank c, or 1024 where no such point exists; each owner row 0 .. 1023 appears exactly once for each (g, o).
All inputs are finite; a program needn't handle non-finite values. No bound on the sum of `local_live` on one device may be relied on, other than what follows from the above.
Results may differ from the reference program's by a relative error of at most 0.017.
Values may be sent and summed in bfloat16 or wider, within the bound.
No kernel may reach another device: no remote copies, remote signals or barrier semaphores. Data moves between devices by JAX's collectives and lax.ppermute only.
A program may use at most 64 MiB of HBM per device.

```python
import math
from functools import partial
import jax
import jax.numpy as jnp
from jax import lax

D = 256
HEADS = 8
HEAD = 32
MLP = 1024
BALL = 256
TILE = 128
RIM = 128
SRC_BLOCKS = 3
LAYERS = 2
PTS_DEV = 1024
POINTS = 32768
BLOCKS = 8
CAP = 512
N_GRP = 8
N_ROT = 4


def draw_features(key, part):
    first_key, row_key, col_key = jax.random.split(jax.random.fold_in(key, 11), 3)
    base = jnp.clip(jax.random.normal(first_key, (POINTS, D)), -6.0, 6.0)
    row_scale = jnp.exp(jax.random.uniform(row_key, (POINTS, 1), minval=math.log(0.3), maxval=math.log(3.0)))
    col_scale = jnp.exp(jax.random.uniform(col_key, (1, D), minval=math.log(0.3), maxval=math.log(3.0)))
    values = base * row_scale * col_scale
    return jnp.clip(values, -64.0, 64.0).astype(jnp.bfloat16)


def qkv_weight(key):
    base = jnp.clip(jax.random.normal(key, (D, 3 * D)), -6.0, 6.0) / math.sqrt(D)
    return jnp.clip(base, -32.0, 32.0).astype(jnp.bfloat16)


def draw_w_ball_qkv(key, part):
    return qkv_weight(jax.random.fold_in(key, 21))


def draw_w_rot_qkv(key, part):
    return qkv_weight(jax.random.fold_in(key, 22))


def relay_tables(key):

    def one_group(group_key):
        count_key, send_key, owner_key = jax.random.split(group_key, 3)
        base_count = (PTS_DEV - CAP) // (N_ROT - 1)
        extra_count = PTS_DEV - CAP - base_count * (N_ROT - 1)
        shuffled = jax.random.permutation(count_key, N_ROT - 1).astype(jnp.int32)
        light_counts = base_count + (shuffled < extra_count).astype(jnp.int32)
        by_distance = jnp.concatenate([light_counts[:1], jnp.full((1,), CAP, jnp.int32), light_counts[1:]])
        member_ids = jnp.arange(N_ROT, dtype=jnp.int32)
        counts = by_distance[(member_ids[None, :] - member_ids[:, None]) % N_ROT]
        end_marks = jnp.cumsum(counts, axis=1)
        start_marks = end_marks - counts
        positions = jax.vmap(lambda sub_key: jax.random.permutation(sub_key, PTS_DEV))(jax.random.split(send_key, N_ROT)).astype(jnp.int32)
        send_peers = jnp.sum((positions[:, :, None] >= end_marks[:, None, :]).astype(jnp.int32), axis=2)
        send_ranks = positions - jnp.take_along_axis(start_marks, send_peers, axis=1)
        offsets = jnp.cumsum(counts, axis=0) - counts
        owner_perm = jax.vmap(lambda sub_key: jax.random.permutation(sub_key, PTS_DEV))(jax.random.split(owner_key, N_ROT)).astype(jnp.int32)
        places = jnp.arange(CAP, dtype=jnp.int32)
        flat_index = offsets.T[:, :, None] + places[None, None, :]
        valid_slot = places[None, None, :] < counts.T[:, :, None]
        looked = jnp.take_along_axis(owner_perm, jnp.minimum(flat_index, PTS_DEV - 1).reshape(N_ROT, -1), axis=1).reshape(N_ROT, N_ROT, CAP)
        inbox_rows = jnp.where(valid_slot, looked, PTS_DEV).astype(jnp.int32)
        return (send_peers, send_ranks, inbox_rows)
    group_keys = jax.random.split(jax.random.fold_in(key, 7), N_GRP)
    return jax.vmap(one_group)(group_keys)


def draw_relay_peer(key, part):
    return relay_tables(key)[0]


def draw_relay_rank(key, part):
    return relay_tables(key)[1]


def draw_relay_inbox(key, part):
    return relay_tables(key)[2]


def touch_ends(values, rng, smallest, largest):
    longest = values.shape.index(max(values.shape))
    spots = []
    for shift in (0, 1):
        where = [jax.random.randint(jax.random.fold_in(rng, axis), (), 0, length) for axis, length in enumerate(values.shape)]
        where[longest] = (where[longest] + shift) % values.shape[longest]
        spots.append(tuple(where))
    return values.at[spots[0]].set(smallest).at[spots[1]].set(largest)


def steps_of(rng, extent, pieces, low, largest):
    def one(axis_at, blocks):
        draws = jax.random.uniform(jax.random.fold_in(jax.random.fold_in(rng, 6), axis_at), (blocks,), jnp.float32, low / len(pieces), largest / len(pieces))
        return jnp.repeat(jnp.exp(draws), extent[axis_at] // blocks).reshape((-1,) + (1,) * (len(extent) - axis_at - 1))

    loudness = one(*pieces[0])
    for cut in pieces[1:]:
        loudness = loudness * one(*cut)
    return loudness


def noise(key, extent, deviation, reach, pieces=(), kind=jnp.bfloat16):
    result = deviation * jax.random.normal(key, extent, jnp.float32)
    if pieces:
        result = result * steps_of(key, extent, pieces, -0.22, 0.18)
    return jnp.clip(result, -reach, reach).astype(kind)


def setup_inputs(seed: int = 0) -> dict:
    key_list = jax.random.split(jax.random.key(seed), 20)
    return {
        "features": draw_features(jax.random.fold_in(key_list[19], 71), 0),
        "w_msg": noise(key_list[1], (LAYERS, D, D), D ** -0.5, 0.375),
        "w_upd": noise(key_list[2], (LAYERS, D, D), D ** -0.5, 0.375),
        "local_tiles": noise(key_list[3], (N_GRP, N_ROT, BLOCKS, SRC_BLOCKS, TILE, TILE), (TILE * (SRC_BLOCKS + 1)) ** -0.5, 0.25, ((0, 8), (1, 4))),
        "local_src": touch_ends(jax.random.randint(key_list[4], (N_GRP, N_ROT, BLOCKS, SRC_BLOCKS), 0, BLOCKS), jax.random.fold_in(key_list[4], 1), 0, BLOCKS - 1).astype(jnp.int32),
        "local_live": touch_ends((jax.random.randint(key_list[5], (N_GRP, N_ROT, BLOCKS, SRC_BLOCKS), 0, 4) < 3).astype(jnp.int32), jax.random.fold_in(key_list[5], 1), 0, 1),
        "border_tiles": noise(key_list[6], (N_GRP, N_ROT, 4, TILE, RIM), (TILE * (SRC_BLOCKS + 1)) ** -0.5, 0.25, ((0, 8), (1, 4))),
        "border_rows": touch_ends(jax.random.randint(key_list[7], (N_GRP, N_ROT, 4, RIM), 0, PTS_DEV), jax.random.fold_in(key_list[7], 1), 0, PTS_DEV - 1).astype(jnp.int32),
        "border_block": touch_ends(jax.random.randint(key_list[8], (N_GRP, N_ROT, 4), 0, BLOCKS), jax.random.fold_in(key_list[8], 1), 0, BLOCKS - 1).astype(jnp.int32),
        "ball_order": jax.vmap(lambda own: jax.random.permutation(own, PTS_DEV))(jax.random.split(key_list[9], N_GRP * N_ROT)).reshape((N_GRP, N_ROT, PTS_DEV)).astype(jnp.int32),
        "w_ball_qkv": draw_w_ball_qkv(jax.random.fold_in(key_list[19], 71), 0),
        "w_ball_out": noise(key_list[11], (D, D), D ** -0.5, 0.375),
        "w_mlp_in": noise(key_list[12], (D, MLP), D ** -0.5, 0.375),
        "w_mlp_out": noise(key_list[13], (MLP, D), MLP ** -0.5, 0.1875),
        "w_rot_qkv": draw_w_rot_qkv(jax.random.fold_in(key_list[19], 71), 0),
        "w_rot_out": noise(key_list[15], (D, D), D ** -0.5, 0.375),
        "relay_peer": draw_relay_peer(jax.random.fold_in(key_list[19], 71), 0),
        "relay_rank": draw_relay_rank(jax.random.fold_in(key_list[19], 71), 0),
        "relay_inbox": draw_relay_inbox(jax.random.fold_in(key_list[19], 71), 0),
    }


EPSILON = 1e-06

def normed(values):
    return values * lax.rsqrt(lax.optimization_barrier(jnp.mean(values * values, axis=-1, keepdims=True)) + EPSILON)

def attend(rows_in, weight_qkv, weight_out):
    joined = jnp.dot(rows_in, weight_qkv, preferred_element_type=jnp.float32).astype(jnp.bfloat16)
    balls = rows_in.shape[0] // BALL
    query = joined[:, :D].reshape(balls, BALL, HEADS, HEAD).astype(jnp.float32)
    keys_all = joined[:, D:2 * D].reshape(balls, BALL, HEADS, HEAD).astype(jnp.float32)
    values_all = joined[:, 2 * D:].reshape(balls, BALL, HEADS, HEAD).astype(jnp.float32)
    scores = jnp.einsum('bqhe,bkhe->bhqk', query, keys_all) / math.sqrt(HEAD)
    weights = jax.nn.softmax(scores, axis=-1).astype(jnp.bfloat16)
    mixed = jnp.einsum('bhqk,bkhe->bqhe', weights.astype(jnp.float32), values_all).astype(jnp.bfloat16)
    return jnp.dot(mixed.reshape(-1, D), weight_out, preferred_element_type=jnp.float32)

def message_device(state, messages, received, edge_tiles, edge_source, edge_live, rim_tiles, rim_block, weight_out):
    blocks_count = state.shape[0] // TILE
    blocks = messages.reshape(blocks_count, TILE, D)
    sources = jnp.take(blocks, edge_source, axis=0) * edge_live[:, :, None, None].astype(jnp.bfloat16)
    gathered = jnp.einsum('bkij,bkjd->bid', edge_tiles.astype(jnp.float32), sources.astype(jnp.float32))
    border = jnp.einsum('jik,jkd->jid', rim_tiles.astype(jnp.float32), received.astype(jnp.float32))
    one_hot = (rim_block[None, :] == jnp.arange(blocks_count)[:, None]).astype(jnp.float32)
    gathered = gathered + jnp.einsum('bj,jid->bid', one_hot, border, precision=lax.Precision.HIGHEST)
    hidden = jax.nn.gelu(gathered.reshape(-1, D)).astype(jnp.bfloat16)
    return state + jnp.dot(hidden, weight_out, preferred_element_type=jnp.float32)

def reference(features, w_msg, w_upd, local_tiles, local_src, local_live, border_tiles, border_rows, border_block, ball_order, w_ball_qkv, w_ball_out, w_mlp_in, w_mlp_out, w_rot_qkv, w_rot_out, relay_peer, relay_rank, relay_inbox):
    state = features.astype(jnp.float32).reshape(N_GRP, N_ROT, PTS_DEV, D)
    for layer_index in range(w_msg.shape[0]):
        weight_in = w_msg[layer_index]
        weight_out = w_upd[layer_index]

        def project(group_state):
            flat_rows = normed(group_state).astype(jnp.bfloat16).reshape(-1, D)
            return jnp.dot(flat_rows, weight_in, preferred_element_type=jnp.float32).astype(jnp.bfloat16).reshape(N_ROT, PTS_DEV, D)
        messages = lax.map(project, state)
        picked = jax.vmap(jax.vmap(lambda block_rows, row_ids: block_rows[row_ids]))(messages, border_rows)
        zero_grp = jnp.zeros_like(picked[:1, :, 0])
        zero_rot = jnp.zeros_like(picked[:, :1, 0])
        from_below = jnp.concatenate([zero_grp, picked[:-1, :, 1]], axis=0)
        from_above = jnp.concatenate([picked[1:, :, 0], zero_grp], axis=0)
        from_left = jnp.concatenate([zero_rot, picked[:, :-1, 3]], axis=1)
        from_right = jnp.concatenate([picked[:, 1:, 2], zero_rot], axis=1)
        received = jnp.stack([from_below, from_above, from_left, from_right], axis=2)

        def per_group(group_args):
            return jax.vmap(partial(message_device, weight_out=weight_out))(*group_args)
        state = lax.map(per_group, (state, messages, received, local_tiles, local_src, local_live, border_tiles, border_block))

    def ball_device(device_state, order_rows):
        balled = device_state[order_rows]
        balled = balled + attend(normed(balled).astype(jnp.bfloat16), w_ball_qkv, w_ball_out)
        hidden = jax.nn.gelu(jnp.dot(normed(balled).astype(jnp.bfloat16), w_mlp_in, preferred_element_type=jnp.float32)).astype(jnp.bfloat16)
        balled = balled + jnp.dot(hidden, w_mlp_out, preferred_element_type=jnp.float32)
        return jnp.zeros_like(device_state).at[order_rows].set(balled)
    state = lax.map(lambda group_args: jax.vmap(ball_device)(*group_args), (state, ball_order))

    def relay_group(group_args):
        group_state, peer_rows, rank_rows, inbox_rows = group_args
        relay_input = normed(group_state).astype(jnp.bfloat16)
        slot_index = peer_rows * CAP + rank_rows
        outgoing = jax.vmap(lambda row_values, slot_ids: jnp.zeros((N_ROT * CAP, D), jnp.bfloat16).at[slot_ids].set(row_values))(relay_input, slot_index)
        incoming = jnp.swapaxes(outgoing.reshape(N_ROT, N_ROT, CAP, D), 0, 1)

        def owner_rows(owner_in, owner_inbox):
            owned = jnp.zeros((PTS_DEV + 1, D), jnp.bfloat16).at[owner_inbox.reshape(-1)].set(owner_in.reshape(-1, D))[:PTS_DEV]
            change = attend(owned, w_rot_qkv, w_rot_out).astype(jnp.bfloat16)
            padded = jnp.concatenate([change, jnp.zeros((1, D), jnp.bfloat16)], axis=0)
            return padded[owner_inbox]
        returned = jax.vmap(owner_rows)(incoming, inbox_rows)
        returned = jnp.swapaxes(returned, 0, 1).reshape(N_ROT, N_ROT * CAP, D)
        update = jax.vmap(lambda back_rows, slot_ids: back_rows[slot_ids])(returned, slot_index)
        return group_state + update.astype(jnp.float32)
    state = lax.map(relay_group, (state, relay_peer, relay_rank, relay_inbox))
    return state.reshape(N_GRP * N_ROT * PTS_DEV, D)
```

```python
import math

import jax
import jax.numpy as jnp
from jax import lax
from jax.experimental import pallas as pl
from jax.experimental.pallas import tpu as pltpu
from jax.sharding import PartitionSpec as P

HEADS = 8
BALL = 256
EPSILON = 1e-06
F32 = jnp.float32
BF16 = jnp.bfloat16
LANES = 128


def up_to(count, unit):
    return -(-count // unit) * unit


def dot(left, right):
    return jnp.dot(left, right, preferred_element_type=F32)


def dot_rows(left, right):
    return lax.dot_general(left, right, (((1,), (1,)), ((), ())), preferred_element_type=F32)


def normed(values):
    return values * lax.rsqrt(jnp.mean(values * values, axis=-1, keepdims=True) + EPSILON)


def iota(shape, axis):
    return lax.broadcasted_iota(jnp.int32, shape, axis)


def hot(mask):
    return jnp.where(mask, 1.0, 0.0).astype(BF16)


def column(lane_row):
    return jnp.transpose(jnp.broadcast_to(lane_row, (LANES, LANES)))


def picks(lane_rows, width):
    count = lane_rows.shape[1]
    out = []
    for start in range(0, count, LANES):
        col = column(lane_rows[:, start : start + LANES])
        out.append(
            jnp.concatenate(
                [hot(col == iota((LANES, LANES), 1) + at) for at in range(0, width, LANES)], axis=1
            )
        )
    return jnp.concatenate(out, axis=0)


def places(lane_rows, height):
    return hot(iota((height, lane_rows.shape[1]), 0) == lane_rows)


def attention(rows_in, weight_qkv, store):
    width = rows_in.shape[1]
    head = width // HEADS
    scale = math.log2(math.e) / math.sqrt(head)
    lane_head = iota((1, width), 1) // head
    masks = [hot(lane_head == h) for h in range(HEADS)]
    for at in range(0, rows_in.shape[0], BALL):
        joined = dot(rows_in[at : at + BALL], weight_qkv).astype(BF16)
        query = joined[:, :width]
        keys = joined[:, width : 2 * width]
        values = joined[:, 2 * width :]
        mixed = jnp.zeros((BALL, width), F32)
        for h in range(HEADS):
            scores = dot_rows(query * masks[h], keys)
            top = jnp.max(scores, axis=-1, keepdims=True)
            raw = jnp.exp2((scores - top) * scale)
            weights = raw * (1.0 / jnp.sum(raw, axis=-1, keepdims=True))
            mixed = mixed + dot(weights.astype(BF16), values * masks[h])
        store(at, mixed.astype(BF16))


def gelu(values):
    inner = math.sqrt(2.0 / math.pi) * (values + 0.044715 * (values * values * values))
    return 0.5 * values * (1.0 + jnp.tanh(inner))


def make_rims(messages, rim_rows_ref, out_refs):
    par_grp = lax.rem(lax.axis_index("grp"), 2)
    par_rot = lax.rem(lax.axis_index("rot"), 2)
    sides = (1 - par_grp, par_grp, 3 - par_rot, 2 + par_rot)
    for side, out in zip(sides, out_refs):
        out[...] = dot(picks(rim_rows_ref[0, 0, pl.ds(side, 1), :], messages.shape[0]), messages).astype(BF16)


def first_kernel(features, w_msg, rim_rows, messages_out, *rims_out):
    messages = dot(normed(features[...].astype(F32)).astype(BF16), w_msg[0]).astype(BF16)
    messages_out[...] = messages
    make_rims(messages, rim_rows, rims_out)


def local_kernel(messages, tiles, source, live, aggregate):
    tile = tiles.shape[-1]
    blocks, sources = tiles.shape[2], tiles.shape[3]
    for b in range(blocks):
        total = None
        for k in range(sources):
            rows = messages[pl.ds(pl.multiple_of(source[0, 0, b, k] * tile, tile), tile), :]
            weight = tiles[0, 0, b, k] * live[0, 0, b, k].astype(BF16)
            part = dot(weight, rows)
            total = part if total is None else total + part
        aggregate[b * tile : (b + 1) * tile, :] = total


def add_border(total, received, tiles, block):
    grp, rot = lax.axis_index("grp"), lax.axis_index("rot")
    par_grp, par_rot = lax.rem(grp, 2), lax.rem(rot, 2)
    sides = (1 - par_grp, par_grp, 3 - par_rot, 2 + par_rot)
    size = tiles.shape[-2]
    for side, rows in zip(sides, received):
        index = jnp.where(side < 2, grp, rot)
        count = jnp.where(side < 2, lax.axis_size("grp"), lax.axis_size("rot"))
        above = lax.rem(side, 2) == 1
        inside = jnp.where(above, index + 1 < count, index > 0)
        part = dot(tiles[0, 0, pl.ds(side, 1)][0], rows[...]) * inside.astype(F32)
        at = pl.ds(pl.multiple_of(block[0, 0, side] * size, size), size)
        total[at, :] += part


def middle_kernel(
    state, aggregate, rec0, rec1, rec2, rec3, tiles, block, w_msg, w_upd, rim_rows,
    state_out, messages_out, rim0, rim1, rim2, rim3, total,
):
    total[...] = aggregate[...]
    add_border(total, (rec0, rec1, rec2, rec3), tiles, block)
    new = state[...].astype(F32) + dot(gelu(total[...]).astype(BF16), w_upd[0])
    state_out[...] = new
    messages = dot(normed(new).astype(BF16), w_msg[1]).astype(BF16)
    messages_out[...] = messages
    make_rims(messages, rim_rows, (rim0, rim1, rim2, rim3))


def slot_of(peer, rank, me, members, capacity, light):
    away = lax.rem(peer - me + members, members)
    base = jnp.where(away == 1, 0, capacity + light * jnp.where(away == 0, 0, away - 1))
    return base + rank


def ball_kernel(
    state, aggregate, rec0, rec1, rec2, rec3, tiles, block, w_upd, order,
    w_qkv, w_out, w_in, w_mlp_out, peer, rank, state_out, *refs, members, capacity, light,
):
    *outgoing, total, mixed = refs
    total[...] = aggregate[...]
    add_border(total, (rec0, rec1, rec2, rec3), tiles, block)
    points = state.shape[0]
    new = state[...] + dot(gelu(total[...]).astype(BF16), w_upd[1])
    unit = normed(new).astype(BF16)
    balled = dot(picks(order[0], points), unit).astype(BF16)

    def store(at, value):
        mixed[at : at + BALL, :] = value

    attention(balled, w_qkv[...], store)
    back = dot(places(order[0], points), mixed[...]).astype(BF16)
    new = new + dot(back, w_out[...])
    hidden = gelu(dot(normed(new).astype(BF16), w_in[...])).astype(BF16)
    new = new + dot(hidden, w_mlp_out[...])
    state_out[...] = new
    me = lax.axis_index("rot")
    slots = slot_of(peer[0], rank[0], me, members, capacity, light)
    unit = normed(new).astype(BF16)
    total_slots = capacity + (members - 1) * light
    sent = dot(places(slots, total_slots), unit).astype(BF16)
    outgoing[0][...] = sent[:capacity]
    for j in range(1, members):
        at = capacity + (j - 1) * light
        outgoing[j][...] = sent[at : at + light]


def senders(members):
    return [1, 0] + list(range(2, members))


def owner_kernel(inbox, w_qkv, *refs, members, capacity, light, wide):
    incoming, returned = refs[:members], refs[members : 2 * members]
    rows_in, mixed = refs[2 * members :]
    me = lax.axis_index("rot")
    points = mixed.shape[0]
    indices = []
    rows_in[...] = jnp.zeros_like(rows_in)
    at = 0
    for away, rows in zip(senders(members), incoming):
        height = capacity if away == 1 else light
        span = capacity if away == 1 else wide
        sender = lax.rem(me - away + members, members)
        rows_in[at : at + height, :] = rows[...]
        indices.append(inbox[0, 0, pl.ds(sender, 1), :][:, :span])
        at += span
    owned = dot(places(jnp.concatenate(indices, axis=1), points), rows_in[...]).astype(BF16)

    def store(at, value):
        mixed[at : at + BALL, :] = value

    attention(owned, w_qkv[...], store)
    for index, out in zip(indices, returned):
        out[...] = dot(picks(index, points), mixed[...])[: out.shape[0]].astype(BF16)


def last_kernel(state, peer, rank, w_out, *refs, members, capacity, light, wide):
    returned, out, rows_in = refs[:members], refs[members], refs[members + 1]
    me = lax.axis_index("rot")
    rows_in[...] = jnp.zeros_like(rows_in)
    at = 0
    for away, rows in zip(senders(members), returned):
        height = capacity if away == 1 else light
        rows_in[at : at + height, :] = rows[...]
        at += capacity if away == 1 else wide
    slots = slot_of(peer[0], rank[0], me, members, capacity, wide)
    update = dot(picks(slots, rows_in.shape[0]), rows_in[...]).astype(BF16)
    out[...] = state[...] + dot(update, w_out[...])


VMEM = pl.BlockSpec(memory_space=pltpu.VMEM)
SMEM = pl.BlockSpec(memory_space=pltpu.SMEM)


def call(kernel, args, outs, scalars=(), scratch=(), flops=0, name=None):
    return pl.pallas_call(
        kernel,
        out_shape=[jax.ShapeDtypeStruct(shape, kind) for shape, kind in outs],
        in_specs=[SMEM if i in scalars else VMEM for i in range(len(args))],
        out_specs=[VMEM] * len(outs),
        scratch_shapes=[pltpu.VMEM(shape, kind) for shape, kind in scratch],
        compiler_params=pltpu.CompilerParams(vmem_limit_bytes=48 * 1024 * 1024),
        cost_estimate=pl.CostEstimate(flops=flops, bytes_accessed=1 << 20, transcendentals=0),
        name=name,
    )(*args)


def swaps(axis, first):
    n_grp, n_rot = lax.axis_size("grp"), lax.axis_size("rot")
    count = n_grp if axis == "grp" else n_rot
    partner = {i: i for i in range(count)}
    for low in range(first, count - 1, 2):
        partner[low], partner[low + 1] = low + 1, low
    if axis == "rot" and first == 1 and count % 2 == 0:
        partner[0], partner[count - 1] = count - 1, 0
    out = []
    for g in range(n_grp):
        for r in range(n_rot):
            to = (partner[g], r) if axis == "grp" else (g, partner[r])
            if to == (g, r) and axis == "grp" and n_rot % 2 == 0:
                to = (g, r ^ 1)
            out.append((g * n_rot + r, to[0] * n_rot + to[1]))
    return out


def exchange(rims):
    plan = [swaps("grp", 0), swaps("grp", 1), swaps("rot", 0), swaps("rot", 1)]
    moved = [None] * 4
    for i in (1, 0, 3, 2):
        moved[i] = lax.ppermute(rims[i], ("grp", "rot"), plan[i])
    return moved


def relay(parts, members, back):
    moved = []
    for away, rows in zip(senders(members), parts):
        if away == 0:
            moved.append(rows)
            continue
        step = members - away if back else away
        moved.append(lax.ppermute(rows, "rot", [(i, (i + step) % members) for i in range(members)]))
    return moved


def local(
    features, w_msg, w_upd, local_tiles, local_src, local_live, border_tiles, border_rows,
    border_block, ball_order, w_ball_qkv, w_ball_out, w_mlp_in, w_mlp_out, w_rot_qkv,
    w_rot_out, relay_peer, relay_rank, relay_inbox,
):
    points, width = features.shape
    members, capacity = lax.axis_size("rot"), relay_inbox.shape[-1]
    rim = border_rows.shape[-1]
    most = up_to(points - capacity, members - 1) // (members - 1)
    light, wide = up_to(most, 16), up_to(most, LANES)
    rims_shape = [((rim, width), BF16)] * 4
    grid, grid16 = ((points, width), F32), ((points, width), BF16)

    messages, *rims = call(
        first_kernel, (features, w_msg, border_rows), [grid16] + rims_shape, name="first_messages"
    )
    received = exchange(rims)
    (aggregate,) = call(
        local_kernel, (messages, local_tiles, local_src, local_live), [grid], scalars=(2, 3),
        name="local_edges",
    )
    state, messages, *rims = call(
        middle_kernel,
        (features, aggregate, *received, border_tiles, border_block, w_msg, w_upd, border_rows),
        [grid, grid16] + rims_shape, scalars=(7,), scratch=[grid], name="second_messages",
    )
    received = exchange(rims)
    (aggregate,) = call(
        local_kernel, (messages, local_tiles, local_src, local_live), [grid], scalars=(2, 3),
        name="local_edges_again",
    )
    sizes = dict(members=members, capacity=capacity, light=light)
    part_shapes = [((capacity, width), BF16)] + [((light, width), BF16)] * (members - 1)

    def bound(kernel, **kw):
        return lambda *refs: kernel(*refs, **kw)

    state, *parts = call(
        bound(ball_kernel, **sizes),
        (
            state, aggregate, *received, border_tiles, border_block, w_upd, ball_order,
            w_ball_qkv, w_ball_out, w_mlp_in, w_mlp_out, relay_peer, relay_rank,
        ),
        [grid] + part_shapes, scalars=(7,), scratch=[grid, grid16], name="ball_layer",
    )
    parts = relay(parts, members, False)
    rows_in = ((capacity + (members - 1) * wide, width), BF16)
    parts = call(
        bound(owner_kernel, wide=wide, **sizes), (relay_inbox, w_rot_qkv, *parts), part_shapes,
        scratch=[rows_in, grid16], name="owner_layer",
    )
    parts = relay(parts, members, True)
    (out,) = call(
        bound(last_kernel, wide=wide, **sizes), (state, relay_peer, relay_rank, w_rot_out, *parts),
        [grid], scratch=[rows_in], name="relayed_changes",
    )
    return out


def solution(mesh):
    table = P("grp", "rot", None)
    in_specs = (
        P(("grp", "rot"), None), P(), P(),
        P("grp", "rot", None, None, None, None),
        P("grp", "rot", None, None), P("grp", "rot", None, None),
        P("grp", "rot", None, None, None),
        P("grp", "rot", None, None), table, table,
        P(), P(), P(), P(), P(), P(),
        table, table, P("grp", "rot", None, None),
    )
    out_specs = P(("grp", "rot"), None)
    return jax.shard_map(local, mesh=mesh, in_specs=in_specs, out_specs=out_specs, check_vma=False)
```

```python
import math

import jax
import jax.numpy as jnp
from jax import lax
from jax.experimental import pallas as pl
from jax.experimental.pallas import tpu as pltpu
from jax.sharding import PartitionSpec as P

HEADS = 8
BALL = 256
EPSILON = 1e-06
F32 = jnp.float32
BF16 = jnp.bfloat16
LANES = 128


def up_to(count, unit):
    return -(-count // unit) * unit


def dot(left, right):
    return jnp.dot(left, right, preferred_element_type=F32)


def dot_rows(left, right):
    return lax.dot_general(left, right, (((1,), (1,)), ((), ())), preferred_element_type=F32)


def normed(values):
    return values * lax.rsqrt(jnp.mean(values * values, axis=-1, keepdims=True) + EPSILON)


def iota(shape, axis):
    return lax.broadcasted_iota(jnp.int32, shape, axis)


def hot(mask):
    return jnp.where(mask, 1.0, 0.0).astype(BF16)


def column(lane_row):
    return jnp.transpose(jnp.broadcast_to(lane_row, (LANES, LANES)))


def columns(lane_rows):
    count = lane_rows.shape[1]
    return jnp.concatenate([column(lane_rows[:, at : at + LANES]) for at in range(0, count, LANES)], axis=0)


def picks_by(cols, width):
    lane = iota(cols.shape, 1)
    return jnp.concatenate([hot(cols == lane + at) for at in range(0, width, LANES)], axis=1)


def picks(lane_rows, width):
    return picks_by(columns(lane_rows), width)


def places(lane_rows, height):
    return hot(iota((height, lane_rows.shape[1]), 0) == lane_rows)


def attention(rows_in, weight_qkv, store):
    width = rows_in.shape[1]
    head = width // HEADS
    scale = math.log2(math.e) / math.sqrt(head)
    lane_head = iota((1, width), 1) // head
    masks = [hot(lane_head == h) for h in range(HEADS)]
    joined = dot(rows_in, weight_qkv).astype(BF16)

    def mix(ball, weights, values):
        spread = jnp.concatenate([values * mask for mask in masks], axis=0)
        store(ball, dot(jnp.concatenate(weights, axis=1), spread).astype(BF16))

    pending = None
    for ball in range(rows_in.shape[0] // BALL):
        own = joined[ball * BALL : (ball + 1) * BALL]
        query, keys, values = own[:, :width], own[:, width : 2 * width], own[:, 2 * width :]
        weights = []
        for h in range(HEADS):
            scores = dot_rows(query * masks[h], keys)
            top = jnp.max(scores, axis=-1, keepdims=True)
            raw = jnp.exp2((scores - top) * scale)
            weights.append((raw * (1.0 / jnp.sum(raw, axis=-1, keepdims=True))).astype(BF16))
        if pending is not None:
            mix(*pending)
        pending = (ball, weights, values)
    mix(*pending)


def gelu(values):
    root = math.sqrt(2.0 / math.pi)
    inner = values * (root + (root * 0.044715) * (values * values))
    return values * (0.5 + 0.5 * jnp.tanh(inner))


def rim_kernel(rim_rows, chosen):
    par_grp, par_rot = lax.rem(lax.axis_index("grp"), 2), lax.rem(lax.axis_index("rot"), 2)
    for at, side in enumerate((1 - par_grp, par_grp, 3 - par_rot, 2 + par_rot)):
        chosen[at] = columns(rim_rows[0, 0, pl.ds(side, 1), :])


def make_rims(messages, chosen, out_refs):
    for at, out in enumerate(out_refs):
        out[...] = dot(picks_by(chosen[at], messages.shape[0]), messages).astype(BF16)


def first_kernel(chosen, features, w_msg, messages_out, *rims_out):
    messages = dot(normed(features[...].astype(F32)).astype(BF16), w_msg[0]).astype(BF16)
    messages_out[...] = messages
    make_rims(messages, chosen, rims_out)


def local_kernel(messages, tiles, source, live, aggregate):
    tile = tiles.shape[-1]
    blocks, sources = tiles.shape[2], tiles.shape[3]
    for b in range(blocks):
        total = None
        for k in range(sources):
            rows = messages[pl.ds(pl.multiple_of(source[0, 0, b, k] * tile, tile), tile), :]
            weight = tiles[0, 0, b, k] * live[0, 0, b, k].astype(BF16)
            part = dot(weight, rows)
            total = part if total is None else total + part
        aggregate[b * tile : (b + 1) * tile, :] = total


def add_border(total, received, tiles, block):
    grp, rot = lax.axis_index("grp"), lax.axis_index("rot")
    par_grp, par_rot = lax.rem(grp, 2), lax.rem(rot, 2)
    sides = (1 - par_grp, par_grp, 3 - par_rot, 2 + par_rot)
    size = tiles.shape[-2]
    for side, rows in zip(sides, received):
        index = jnp.where(side < 2, grp, rot)
        count = jnp.where(side < 2, lax.axis_size("grp"), lax.axis_size("rot"))
        above = lax.rem(side, 2) == 1
        inside = jnp.where(above, index + 1 < count, index > 0)
        part = dot(tiles[0, 0, pl.ds(side, 1)][0], rows[...]) * inside.astype(F32)
        at = pl.ds(pl.multiple_of(block[0, 0, side] * size, size), size)
        total[at, :] += part


def middle_kernel(
    state, aggregate, rec0, rec1, rec2, rec3, tiles, block, w_msg, w_upd, chosen,
    state_out, messages_out, rim0, rim1, rim2, rim3, total,
):
    total[...] = aggregate[...]
    add_border(total, (rec0, rec1, rec2, rec3), tiles, block)
    new = state[...].astype(F32) + dot(gelu(total[...]).astype(BF16), w_upd[0])
    state_out[...] = new
    messages = dot(normed(new).astype(BF16), w_msg[1]).astype(BF16)
    messages_out[...] = messages
    make_rims(messages, chosen, (rim0, rim1, rim2, rim3))


def slot_of(peer, rank, me, members, capacity, light):
    away = lax.rem(peer - me + members, members)
    base = jnp.where(away == 1, 0, capacity + light * jnp.where(away == 0, 0, away - 1))
    return base + rank


def ball_kernel(
    state, aggregate, rec0, rec1, rec2, rec3, tiles, block, w_upd, order, w_qkv,
    state_out, mixed, total,
):
    total[...] = aggregate[...]
    add_border(total, (rec0, rec1, rec2, rec3), tiles, block)
    points = state.shape[0]
    new = state[...] + dot(gelu(total[...]).astype(BF16), w_upd[1])
    state_out[...] = new
    unit = normed(new).astype(BF16)
    balled = [
        dot(picks(order[0][:, at : at + BALL], points), unit).astype(BF16)
        for at in range(0, points, BALL)
    ]

    def store(ball, value):
        mixed[ball * BALL : (ball + 1) * BALL, :] = value

    attention(jnp.concatenate(balled, axis=0), w_qkv[...], store)


def feed_kernel(
    state, mixed, order, w_out, w_in, w_mlp_out, peer, rank, state_out, *outgoing,
    members, capacity, light,
):
    points = state.shape[0]
    back = dot(places(order[0], points), mixed[...]).astype(BF16)
    starts = range(0, points, BALL)
    pieces = [state[at : at + BALL, :] + dot(back[at : at + BALL], w_out[...]) for at in starts]
    inner = [dot(normed(piece).astype(BF16), w_in[...]) for piece in pieces]
    units = []
    for at, piece, values in zip(starts, pieces, inner):
        piece = piece + dot(gelu(values).astype(BF16), w_mlp_out[...])
        state_out[at : at + BALL, :] = piece
        units.append(normed(piece).astype(BF16))
    me = lax.axis_index("rot")
    slots = slot_of(peer[0], rank[0], me, members, capacity, light)
    total_slots = capacity + (members - 1) * light
    sent = dot(places(slots, total_slots), jnp.concatenate(units, axis=0)).astype(BF16)
    outgoing[0][...] = sent[:capacity]
    for j in range(1, members):
        at = capacity + (j - 1) * light
        outgoing[j][...] = sent[at : at + light]


def senders(members):
    return [1, 0] + list(range(2, members))


def owner_kernel(inbox, w_qkv, *refs, members, capacity, light, wide):
    incoming, returned = refs[:members], refs[members : 2 * members]
    rows_in, mixed = refs[2 * members :]
    me = lax.axis_index("rot")
    points = mixed.shape[0]
    indices = []
    at = 0
    for away, rows in zip(senders(members), incoming):
        height = capacity if away == 1 else light
        span = capacity if away == 1 else wide
        sender = lax.rem(me - away + members, members)
        rows_in[at : at + height, :] = rows[...]
        if span > height:
            rows_in[at + height : at + span, :] = jnp.zeros((span - height, rows_in.shape[1]), BF16)
        indices.append(inbox[0, 0, pl.ds(sender, 1), :][:, :span])
        at += span
    index_row = jnp.concatenate(indices, axis=1)
    owned = dot(places(index_row, points), rows_in[...]).astype(BF16)

    def store(ball, value):
        mixed[ball * BALL : (ball + 1) * BALL, :] = value

    attention(owned, w_qkv[...], store)
    for index, out in zip(indices, returned):
        out[...] = dot(picks(index, points), mixed[...])[: out.shape[0]].astype(BF16)


def last_kernel(state, peer, rank, w_out, *refs, members, capacity, light, wide):
    returned, out, rows_in = refs[:members], *refs[members:]
    me = lax.axis_index("rot")
    at = 0
    for away, rows in zip(senders(members), returned):
        height = capacity if away == 1 else light
        span = capacity if away == 1 else wide
        rows_in[at : at + height, :] = rows[...]
        if span > height:
            rows_in[at + height : at + span, :] = jnp.zeros((span - height, rows_in.shape[1]), BF16)
        at += span
    slots = slot_of(peer[0], rank[0], me, members, capacity, wide)
    update = dot(picks(slots, rows_in.shape[0]), rows_in[...]).astype(BF16)
    out[...] = state[...] + dot(update, w_out[...])


VMEM = pl.BlockSpec(memory_space=pltpu.VMEM)
SMEM = pl.BlockSpec(memory_space=pltpu.SMEM)


def call(kernel, args, outs, scalars=(), scratch=(), flops=0, moved=1 << 20, name=None):
    return pl.pallas_call(
        kernel,
        out_shape=[jax.ShapeDtypeStruct(shape, kind) for shape, kind in outs],
        in_specs=[SMEM if i in scalars else VMEM for i in range(len(args))],
        out_specs=[VMEM] * len(outs),
        scratch_shapes=[pltpu.VMEM(shape, kind) for shape, kind in scratch],
        compiler_params=pltpu.CompilerParams(vmem_limit_bytes=48 * 1024 * 1024),
        cost_estimate=pl.CostEstimate(flops=flops, bytes_accessed=moved, transcendentals=0),
        name=name,
    )(*args)


def bound(kernel, **kw):
    return lambda *refs: kernel(*refs, **kw)


def swaps(axis, first):
    n_grp, n_rot = lax.axis_size("grp"), lax.axis_size("rot")
    count = n_grp if axis == "grp" else n_rot
    partner = {i: i for i in range(count)}
    for low in range(first, count - 1, 2):
        partner[low], partner[low + 1] = low + 1, low
    if axis == "rot" and first == 1 and count % 2 == 0:
        partner[0], partner[count - 1] = count - 1, 0
    out = []
    for g in range(n_grp):
        for r in range(n_rot):
            to = (partner[g], r) if axis == "grp" else (g, partner[r])
            if to == (g, r) and axis == "grp" and n_rot % 2 == 0:
                to = (g, r ^ 1)
            out.append((g * n_rot + r, to[0] * n_rot + to[1]))
    return out


def exchange(rims):
    plan = [swaps("grp", 0), swaps("grp", 1), swaps("rot", 0), swaps("rot", 1)]
    moved = [None] * 4
    for i in (1, 0, 3, 2):
        moved[i] = lax.ppermute(rims[i], ("grp", "rot"), plan[i])
    return moved


def relay(parts, members, back):
    moved = list(parts)
    for at, away in reversed(list(enumerate(senders(members)))):
        if away == 0:
            continue
        step = members - away if back else away
        turn = [(i, (i + step) % members) for i in range(members)]
        moved[at] = lax.ppermute(parts[at], "rot", turn)
    return moved


def local(
    features, w_msg, w_upd, local_tiles, local_src, local_live, border_tiles, border_rows,
    border_block, ball_order, w_ball_qkv, w_ball_out, w_mlp_in, w_mlp_out, w_rot_qkv,
    w_rot_out, relay_peer, relay_rank, relay_inbox,
):
    points, width = features.shape
    members, capacity = lax.axis_size("rot"), relay_inbox.shape[-1]
    rim = border_rows.shape[-1]
    most = up_to(points - capacity, members - 1) // (members - 1)
    light, wide = up_to(most, 16), up_to(most, LANES)
    rims_shape = [((rim, width), BF16)] * 4
    grid, grid16 = ((points, width), F32), ((points, width), BF16)

    (chosen,) = call(
        rim_kernel, (border_rows,), [((4, rim, LANES), jnp.int32)], flops=1 << 31,
        moved=1 << 23, name="rim_rows",
    )
    messages, *rims = call(
        first_kernel, (chosen, features, w_msg), [grid16] + rims_shape, name="first_messages"
    )
    received = exchange(rims)
    (aggregate,) = call(
        local_kernel, (messages, local_tiles, local_src, local_live), [grid], scalars=(2, 3),
        name="local_edges",
    )
    state, messages, *rims = call(
        middle_kernel,
        (features, aggregate, *received, border_tiles, border_block, w_msg, w_upd, chosen),
        [grid, grid16] + rims_shape, scalars=(7,), scratch=[grid], name="second_messages",
    )
    received = exchange(rims)
    (aggregate,) = call(
        local_kernel, (messages, local_tiles, local_src, local_live), [grid], scalars=(2, 3),
        name="local_edges_again",
    )
    sizes = dict(members=members, capacity=capacity, light=light)
    part_shapes = [((capacity, width), BF16)] + [((light, width), BF16)] * (members - 1)

    state, mixed = call(
        ball_kernel,
        (
            state, aggregate, *received, border_tiles, border_block, w_upd, ball_order,
            w_ball_qkv,
        ),
        [grid, grid16], scalars=(7,), scratch=[grid], name="ball_attention",
    )
    state, *parts = call(
        bound(feed_kernel, **sizes),
        (state, mixed, ball_order, w_ball_out, w_mlp_in, w_mlp_out, relay_peer, relay_rank),
        [grid] + part_shapes, name="feed_forward",
    )
    parts = relay(parts, members, False)
    rows_in = ((capacity + (members - 1) * wide, width), BF16)
    parts = call(
        bound(owner_kernel, wide=wide, **sizes), (relay_inbox, w_rot_qkv, *parts), part_shapes,
        scratch=[rows_in, grid16], name="owner_layer",
    )
    parts = relay(parts, members, True)
    (out,) = call(
        bound(last_kernel, wide=wide, **sizes), (state, relay_peer, relay_rank, w_rot_out, *parts),
        [grid], scratch=[rows_in], name="relayed_changes",
    )
    return out


def solution(mesh):
    table = P("grp", "rot", None)
    in_specs = (
        P(("grp", "rot"), None), P(), P(),
        P("grp", "rot", None, None, None, None),
        P("grp", "rot", None, None), P("grp", "rot", None, None),
        P("grp", "rot", None, None, None),
        P("grp", "rot", None, None), table, table,
        P(), P(), P(), P(), P(), P(),
        table, table, P("grp", "rot", None, None),
    )
    out_specs = P(("grp", "rot"), None)
    return jax.shard_map(local, mesh=mesh, in_specs=in_specs, out_specs=out_specs, check_vma=False)
```

```python
import math

import jax
import jax.numpy as jnp
from jax import lax
from jax.experimental import pallas as pl
from jax.experimental.pallas import tpu as pltpu
from jax.sharding import PartitionSpec as P

HEADS = 8
BALL = 256
EPSILON = 1e-06
F32 = jnp.float32
BF16 = jnp.bfloat16
LANES = 128


def up_to(count, unit):
    return -(-count // unit) * unit


def dot(left, right):
    return jnp.dot(left, right, preferred_element_type=F32)


def dot_rows(left, right):
    return lax.dot_general(left, right, (((1,), (1,)), ((), ())), preferred_element_type=F32)


def normed(values):
    return values * lax.rsqrt(jnp.mean(values * values, axis=-1, keepdims=True) + EPSILON)


def iota(shape, axis):
    return lax.broadcasted_iota(jnp.int32, shape, axis)


def hot(mask):
    return jnp.where(mask, 1.0, 0.0).astype(BF16)


def column(lane_row):
    return jnp.transpose(jnp.broadcast_to(lane_row, (LANES, LANES)))


def columns(lane_rows):
    count = lane_rows.shape[1]
    return jnp.concatenate([column(lane_rows[:, at : at + LANES]) for at in range(0, count, LANES)], axis=0)


def picks_by(cols, width):
    lane = iota(cols.shape, 1)
    return jnp.concatenate([hot(cols == lane + at) for at in range(0, width, LANES)], axis=1)


def picks(lane_rows, width):
    return picks_by(columns(lane_rows), width)


def places(lane_rows, height):
    return hot(iota((height, lane_rows.shape[1]), 0) == lane_rows)


def attention(rows_in, weight_qkv, store):
    width = rows_in.shape[1]
    head = width // HEADS
    scale = math.log2(math.e) / math.sqrt(head)
    lane_head = iota((1, width), 1) // head
    masks = [hot(lane_head == h) for h in range(HEADS)]
    joined = dot(rows_in, weight_qkv).astype(BF16)

    def mix(ball, weights, values):
        spread = jnp.concatenate([values * mask for mask in masks], axis=0)
        store(ball, dot(jnp.concatenate(weights, axis=1), spread).astype(BF16))

    pending = None
    for ball in range(rows_in.shape[0] // BALL):
        own = joined[ball * BALL : (ball + 1) * BALL]
        query, keys, values = own[:, :width], own[:, width : 2 * width], own[:, 2 * width :]
        weights = []
        for h in range(HEADS):
            scores = dot_rows(query * masks[h], keys)
            top = jnp.max(scores, axis=-1, keepdims=True)
            raw = jnp.exp2((scores - top) * scale)
            weights.append((raw * (1.0 / jnp.sum(raw, axis=-1, keepdims=True))).astype(BF16))
        if pending is not None:
            mix(*pending)
        pending = (ball, weights, values)
    mix(*pending)


def gelu(values):
    root = math.sqrt(2.0 / math.pi)
    inner = values * (root + (root * 0.044715) * (values * values))
    return values * (0.5 + 0.5 * jnp.tanh(inner))


def rim_kernel(rim_rows, chosen):
    par_grp, par_rot = lax.rem(lax.axis_index("grp"), 2), lax.rem(lax.axis_index("rot"), 2)
    for at, side in enumerate((1 - par_grp, par_grp, 3 - par_rot, 2 + par_rot)):
        chosen[at] = columns(rim_rows[0, 0, pl.ds(side, 1), :])


def make_rims(messages, chosen, out_refs):
    for at, out in enumerate(out_refs):
        out[...] = dot(picks_by(chosen[at], messages.shape[0]), messages).astype(BF16)


def first_kernel(chosen, features, w_msg, messages_out, *rims_out):
    messages = dot(normed(features[...].astype(F32)).astype(BF16), w_msg[0]).astype(BF16)
    messages_out[...] = messages
    make_rims(messages, chosen, rims_out)


def slots_kernel(order, peer, rank, after, slots_out, *, members, capacity, light):
    me = lax.axis_index("rot")
    slots = slot_of(peer[0], rank[0], me, members, capacity, light)
    points = slots.shape[1]
    digits = jnp.concatenate([slots // LANES, lax.rem(slots, LANES)] + [jnp.zeros_like(slots)] * 6, axis=0)
    moved = dot(digits.astype(F32).astype(BF16), places(order[0], points)).astype(jnp.int32)
    slots_out[0:1, :] = slots
    slots_out[1:2, :] = moved[0:1] * LANES + moved[1:2]


def local_kernel(messages, tiles, source, live, aggregate):
    tile = tiles.shape[-1]
    blocks, sources = tiles.shape[2], tiles.shape[3]
    for b in range(blocks):
        total = None
        for k in range(sources):
            rows = messages[pl.ds(pl.multiple_of(source[0, 0, b, k] * tile, tile), tile), :]
            weight = tiles[0, 0, b, k] * live[0, 0, b, k].astype(BF16)
            part = dot(weight, rows)
            total = part if total is None else total + part
        aggregate[b * tile : (b + 1) * tile, :] = total


def add_border(total, received, tiles, block):
    grp, rot = lax.axis_index("grp"), lax.axis_index("rot")
    par_grp, par_rot = lax.rem(grp, 2), lax.rem(rot, 2)
    sides = (1 - par_grp, par_grp, 3 - par_rot, 2 + par_rot)
    size = tiles.shape[-2]
    for side, rows in zip(sides, received):
        index = jnp.where(side < 2, grp, rot)
        count = jnp.where(side < 2, lax.axis_size("grp"), lax.axis_size("rot"))
        above = lax.rem(side, 2) == 1
        inside = jnp.where(above, index + 1 < count, index > 0)
        part = dot(tiles[0, 0, pl.ds(side, 1)][0], rows[...]) * inside.astype(F32)
        at = pl.ds(pl.multiple_of(block[0, 0, side] * size, size), size)
        total[at, :] += part


def middle_kernel(
    state, aggregate, rec0, rec1, rec2, rec3, tiles, block, w_msg, w_upd, chosen,
    state_out, messages_out, rim0, rim1, rim2, rim3, total,
):
    total[...] = aggregate[...]
    add_border(total, (rec0, rec1, rec2, rec3), tiles, block)
    new = state[...].astype(F32) + dot(gelu(total[...]).astype(BF16), w_upd[0])
    state_out[...] = new
    messages = dot(normed(new).astype(BF16), w_msg[1]).astype(BF16)
    messages_out[...] = messages
    make_rims(messages, chosen, (rim0, rim1, rim2, rim3))


def slot_of(peer, rank, me, members, capacity, light):
    away = lax.rem(peer - me + members, members)
    base = jnp.where(away == 1, 0, capacity + light * jnp.where(away == 0, 0, away - 1))
    return base + rank


def ball_kernel(
    state, aggregate, rec0, rec1, rec2, rec3, tiles, block, w_upd, order, w_qkv,
    state_out, mixed, total,
):
    total[...] = aggregate[...]
    add_border(total, (rec0, rec1, rec2, rec3), tiles, block)
    points = state.shape[0]
    new = state[...] + dot(gelu(total[...]).astype(BF16), w_upd[1])
    state_out[...] = new
    unit = normed(new).astype(BF16)
    balled = [
        dot(picks(order[0][:, at : at + BALL], points), unit).astype(BF16)
        for at in range(0, points, BALL)
    ]

    def store(ball, value):
        mixed[ball * BALL : (ball + 1) * BALL, :] = value

    attention(jnp.concatenate(balled, axis=0), w_qkv[...], store)


def feed(pieces, w_in, w_mlp_out):
    inner = [dot(normed(piece).astype(BF16), w_in[...]) for piece in pieces]
    return [
        piece + dot(gelu(values).astype(BF16), w_mlp_out[...])
        for piece, values in zip(pieces, inner)
    ]


def sent_kernel(state, mixed, slots, w_out, w_in, w_mlp_out, *refs, start, after):
    outgoing = refs[after:]
    count = sum(out.shape[0] for out in outgoing)
    at_row = hot(iota((count, slots.shape[1]), 0) + start == slots[0:1, :])
    at_ball = hot(iota((count, slots.shape[1]), 0) + start == slots[1:2, :])
    back = dot(at_ball, mixed[...]).astype(BF16)
    rows = dot(at_row, state[...].astype(BF16))
    step = up_to(count // 2, 16)
    cuts = [slice(0, step), slice(step, count)]
    done = feed([rows[cut] + dot(back[cut], w_out[...]) for cut in cuts], w_in, w_mlp_out)
    units = jnp.concatenate([normed(piece).astype(BF16) for piece in done], axis=0)
    at = 0
    for out in outgoing:
        out[...] = units[at : at + out.shape[0]]
        at += out.shape[0]


def kept_kernel(state, mixed, order, w_out, w_in, w_mlp_out, after, state_out):
    points = state.shape[0]
    back = dot(places(order[0], points), mixed[...]).astype(BF16)
    starts = range(0, points, BALL)
    pieces = [state[at : at + BALL, :] + dot(back[at : at + BALL], w_out[...]) for at in starts]
    for at, piece in zip(starts, feed(pieces, w_in, w_mlp_out)):
        state_out[at : at + BALL, :] = piece


def senders(members):
    return [1, 0] + list(range(2, members))


def owner_kernel(inbox, w_qkv, *refs, members, capacity, light, wide):
    incoming, returned = refs[:members], refs[members : 2 * members]
    rows_in, mixed = refs[2 * members :]
    me = lax.axis_index("rot")
    points = mixed.shape[0]
    indices = []
    at = 0
    for away, rows in zip(senders(members), incoming):
        height = capacity if away == 1 else light
        span = capacity if away == 1 else wide
        sender = lax.rem(me - away + members, members)
        rows_in[at : at + height, :] = rows[...]
        if span > height:
            rows_in[at + height : at + span, :] = jnp.zeros((span - height, rows_in.shape[1]), BF16)
        indices.append(inbox[0, 0, pl.ds(sender, 1), :][:, :span])
        at += span
    index_row = jnp.concatenate(indices, axis=1)
    owned = dot(places(index_row, points), rows_in[...]).astype(BF16)

    def store(ball, value):
        mixed[ball * BALL : (ball + 1) * BALL, :] = value

    attention(owned, w_qkv[...], store)
    for index, out in zip(indices, returned):
        out[...] = dot(picks(index, points), mixed[...])[: out.shape[0]].astype(BF16)


def last_kernel(state, peer, rank, w_out, *refs, members, capacity, light, wide):
    returned, out, rows_in = refs[:members], *refs[members:]
    me = lax.axis_index("rot")
    at = 0
    for away, rows in zip(senders(members), returned):
        height = capacity if away == 1 else light
        span = capacity if away == 1 else wide
        rows_in[at : at + height, :] = rows[...]
        if span > height:
            rows_in[at + height : at + span, :] = jnp.zeros((span - height, rows_in.shape[1]), BF16)
        at += span
    slots = slot_of(peer[0], rank[0], me, members, capacity, wide)
    update = dot(picks(slots, rows_in.shape[0]), rows_in[...]).astype(BF16)
    out[...] = state[...] + dot(update, w_out[...])


VMEM = pl.BlockSpec(memory_space=pltpu.VMEM)
SMEM = pl.BlockSpec(memory_space=pltpu.SMEM)


def call(kernel, args, outs, scalars=(), scratch=(), flops=0, moved=1 << 20, name=None):
    return pl.pallas_call(
        kernel,
        out_shape=[jax.ShapeDtypeStruct(shape, kind) for shape, kind in outs],
        in_specs=[SMEM if i in scalars else VMEM for i in range(len(args))],
        out_specs=[VMEM] * len(outs),
        scratch_shapes=[pltpu.VMEM(shape, kind) for shape, kind in scratch],
        compiler_params=pltpu.CompilerParams(vmem_limit_bytes=48 * 1024 * 1024),
        cost_estimate=pl.CostEstimate(flops=flops, bytes_accessed=moved, transcendentals=0),
        name=name,
    )(*args)


def bound(kernel, **kw):
    return lambda *refs: kernel(*refs, **kw)


def swaps(axis, first):
    n_grp, n_rot = lax.axis_size("grp"), lax.axis_size("rot")
    count = n_grp if axis == "grp" else n_rot
    partner = {i: i for i in range(count)}
    for low in range(first, count - 1, 2):
        partner[low], partner[low + 1] = low + 1, low
    if axis == "rot" and first == 1 and count % 2 == 0:
        partner[0], partner[count - 1] = count - 1, 0
    out = []
    for g in range(n_grp):
        for r in range(n_rot):
            to = (partner[g], r) if axis == "grp" else (g, partner[r])
            if to == (g, r) and axis == "grp" and n_rot % 2 == 0:
                to = (g, r ^ 1)
            out.append((g * n_rot + r, to[0] * n_rot + to[1]))
    return out


def exchange(rims):
    plan = [swaps("grp", 0), swaps("grp", 1), swaps("rot", 0), swaps("rot", 1)]
    moved = [None] * 4
    for i in (1, 0, 3, 2):
        moved[i] = lax.ppermute(rims[i], ("grp", "rot"), plan[i])
    return moved


def relay(parts, members, back):
    moved = list(parts)
    for at, away in reversed(list(enumerate(senders(members)))):
        if away == 0:
            continue
        step = members - away if back else away
        turn = [(i, (i + step) % members) for i in range(members)]
        moved[at] = lax.ppermute(parts[at], "rot", turn)
    return moved


def local(
    features, w_msg, w_upd, local_tiles, local_src, local_live, border_tiles, border_rows,
    border_block, ball_order, w_ball_qkv, w_ball_out, w_mlp_in, w_mlp_out, w_rot_qkv,
    w_rot_out, relay_peer, relay_rank, relay_inbox,
):
    points, width = features.shape
    members, capacity = lax.axis_size("rot"), relay_inbox.shape[-1]
    rim = border_rows.shape[-1]
    most = up_to(points - capacity, members - 1) // (members - 1)
    light, wide = up_to(most, 16), up_to(most, LANES)
    rims_shape = [((rim, width), BF16)] * 4
    grid, grid16 = ((points, width), F32), ((points, width), BF16)

    (chosen,) = call(
        rim_kernel, (border_rows,), [((4, rim, LANES), jnp.int32)], flops=1 << 31,
        moved=1 << 23, name="rim_rows",
    )
    sizes = dict(members=members, capacity=capacity, light=light)
    part_shapes = [((capacity, width), BF16)] + [((light, width), BF16)] * (members - 1)

    messages, *rims = call(
        first_kernel, (chosen, features, w_msg), [grid16] + rims_shape, name="first_messages"
    )
    received = exchange(rims)
    (aggregate,) = call(
        local_kernel, (messages, local_tiles, local_src, local_live), [grid], scalars=(2, 3),
        name="local_edges",
    )
    (slots,) = call(
        bound(slots_kernel, **sizes), (ball_order, relay_peer, relay_rank, messages),
        [((2, points), jnp.int32)], name="slots",
    )
    state, messages, *rims = call(
        middle_kernel,
        (features, aggregate, *received, border_tiles, border_block, w_msg, w_upd, chosen),
        [grid, grid16] + rims_shape, scalars=(7,), scratch=[grid], name="second_messages",
    )
    received = exchange(rims)
    (aggregate,) = call(
        local_kernel, (messages, local_tiles, local_src, local_live), [grid], scalars=(2, 3),
        name="local_edges_again",
    )
    state, mixed = call(
        ball_kernel,
        (
            state, aggregate, *received, border_tiles, border_block, w_upd, ball_order,
            w_ball_qkv,
        ),
        [grid, grid16], scalars=(7,), scratch=[grid], name="ball_attention",
    )
    weights = (w_ball_out, w_mlp_in, w_mlp_out)
    heavy = call(
        bound(sent_kernel, start=0, after=0), (state, mixed, slots, *weights), part_shapes[:1],
        name="heavy_rows",
    )
    lighter = call(
        bound(sent_kernel, start=capacity, after=1), (state, mixed, slots, *weights, *heavy),
        part_shapes[1:], name="light_rows",
    )
    parts = [*heavy, *lighter]
    (state,) = call(
        kept_kernel, (state, mixed, ball_order, *weights, lighter[0]), [grid], name="kept_rows",
    )
    parts = relay(parts, members, False)
    rows_in = ((capacity + (members - 1) * wide, width), BF16)
    parts = call(
        bound(owner_kernel, wide=wide, **sizes), (relay_inbox, w_rot_qkv, *parts), part_shapes,
        scratch=[rows_in, grid16], name="owner_layer",
    )
    parts = relay(parts, members, True)
    (out,) = call(
        bound(last_kernel, wide=wide, **sizes), (state, relay_peer, relay_rank, w_rot_out, *parts),
        [grid], scratch=[rows_in], name="relayed_changes",
    )
    return out


def solution(mesh):
    table = P("grp", "rot", None)
    in_specs = (
        P(("grp", "rot"), None), P(), P(),
        P("grp", "rot", None, None, None, None),
        P("grp", "rot", None, None), P("grp", "rot", None, None),
        P("grp", "rot", None, None, None),
        P("grp", "rot", None, None), table, table,
        P(), P(), P(), P(), P(), P(),
        table, table, P("grp", "rot", None, None),
    )
    out_specs = P(("grp", "rot"), None)
    return jax.shard_map(local, mesh=mesh, in_specs=in_specs, out_specs=out_specs, check_vma=False)
```

```python
import math

import jax
import jax.numpy as jnp
from jax import lax
from jax.experimental import pallas as pl
from jax.experimental.pallas import tpu as pltpu
from jax.sharding import PartitionSpec as P

HEADS = 8
BALL = 256
EPSILON = 1e-06
F32 = jnp.float32
BF16 = jnp.bfloat16
LANES = 128
DIGIT = 32


def up_to(count, unit):
    return -(-count // unit) * unit


def dot(left, right):
    return jnp.dot(left, right, preferred_element_type=F32)


def dot_rows(left, right):
    return lax.dot_general(left, right, (((1,), (1,)), ((), ())), preferred_element_type=F32)


def normed(values):
    return values * lax.rsqrt(jnp.mean(values * values, axis=-1, keepdims=True) + EPSILON)


def iota(shape, axis):
    return lax.broadcasted_iota(jnp.int32, shape, axis)


def hot(mask):
    return jnp.where(mask, 1.0, 0.0).astype(BF16)


def column(lane_row):
    return jnp.transpose(jnp.broadcast_to(lane_row, (LANES, LANES)))


def columns(lane_rows):
    count = lane_rows.shape[1]
    return jnp.concatenate([column(lane_rows[:, at : at + LANES]) for at in range(0, count, LANES)], axis=0)


def picks_by(cols, width):
    lane = iota(cols.shape, 1)
    return jnp.concatenate([hot(cols == lane + at) for at in range(0, width, LANES)], axis=1)


def picks(lane_rows, width):
    return picks_by(columns(lane_rows), width)


def places(lane_rows, height):
    return hot(iota((height, lane_rows.shape[1]), 0) == lane_rows)


def attention(rows_in, weight_qkv, store):
    width = rows_in.shape[1]
    head = width // HEADS
    scale = math.log2(math.e) / math.sqrt(head)
    lane_head = iota((1, width), 1) // head
    masks = [hot(lane_head == h) for h in range(HEADS)]
    joined = dot(rows_in, weight_qkv).astype(BF16)

    def mix(ball, weights, values):
        spread = jnp.concatenate([values * mask for mask in masks], axis=0)
        store(ball, dot(jnp.concatenate(weights, axis=1), spread).astype(BF16))

    pending = None
    for ball in range(rows_in.shape[0] // BALL):
        own = joined[ball * BALL : (ball + 1) * BALL]
        query, keys, values = own[:, :width], own[:, width : 2 * width], own[:, 2 * width :]
        weights = []
        for h in range(HEADS):
            near = slice(h * head // LANES * LANES, (h * head // LANES + 1) * LANES)
            scores = dot_rows(query[:, near] * masks[h][:, near], keys[:, near])
            top = jnp.max(scores, axis=-1, keepdims=True)
            raw = jnp.exp2((scores - top) * scale)
            weights.append((raw * (1.0 / jnp.sum(raw, axis=-1, keepdims=True))).astype(BF16))
        if pending is not None:
            mix(*pending)
        pending = (ball, weights, values)
    mix(*pending)


def gelu(values):
    root = math.sqrt(2.0 / math.pi)
    inner = values * (root + (root * 0.044715) * (values * values))
    return values * (0.5 + 0.5 * jnp.tanh(inner))


def rim_kernel(rim_rows, chosen):
    par_grp, par_rot = lax.rem(lax.axis_index("grp"), 2), lax.rem(lax.axis_index("rot"), 2)
    for at, side in enumerate((1 - par_grp, par_grp, 3 - par_rot, 2 + par_rot)):
        chosen[at] = columns(rim_rows[0, 0, pl.ds(side, 1), :])


def make_rims(messages, chosen, out_refs):
    for at, out in enumerate(out_refs):
        out[: chosen.shape[1], :] = dot(picks_by(chosen[at], messages.shape[0]), messages).astype(BF16)


def first_kernel(chosen, features, w_msg, inbox, messages_out, *rims_out):
    points, width = features.shape
    messages = [
        dot(normed(features[at : at + BALL, :].astype(F32)).astype(BF16), w_msg[0]).astype(BF16)
        for at in range(0, points, BALL)
    ]
    messages = jnp.concatenate(messages, axis=0)
    messages_out[...] = messages
    make_rims(messages, chosen, rims_out)
    table = inbox[0, 0]
    pieces = [table[:, at : at + width] for at in range(0, table.shape[1], width)]
    digits = [piece // DIGIT for piece in pieces] + [lax.rem(piece, DIGIT) for piece in pieces]
    digits = jnp.concatenate(digits, axis=0).astype(F32).astype(BF16)
    for out in rims_out[2:]:
        out[chosen.shape[1] :, :] = digits


def slots_kernel(
    order, peer, rank, rec2, rec3, after, slots_out, inbox_out, *, members, capacity, light, rim
):
    me = lax.axis_index("rot")
    slots = slot_of(peer[0], rank[0], me, members, capacity, light)
    points = slots.shape[1]
    digits = jnp.concatenate([slots // LANES, lax.rem(slots, LANES)] + [jnp.zeros_like(slots)] * 6, axis=0)
    moved = dot(digits.astype(F32).astype(BF16), places(order[0], points)).astype(jnp.int32)
    slots_out[0:1, :] = slots
    slots_out[1:2, :] = moved[0:1] * LANES + moved[1:2]
    even = (lax.rem(me, 2) == 0).astype(F32)
    table = rec2[rim:, :].astype(F32) * even + rec3[rim:, :].astype(F32) * (1.0 - even)
    half = table.shape[0] // 2
    table = (table[:half] * DIGIT + table[half:]).astype(jnp.int32)
    width = table.shape[1]
    for at in range(0, capacity, width):
        first = at // width * members
        inbox_out[:, at : at + width] = table[first : first + members]


def local_kernel(messages, tiles, source, live, aggregate):
    tile = tiles.shape[-1]
    blocks, sources = tiles.shape[2], tiles.shape[3]
    for b in range(blocks):
        total = None
        for k in range(sources):
            rows = messages[pl.ds(pl.multiple_of(source[0, 0, b, k] * tile, tile), tile), :]
            weight = tiles[0, 0, b, k] * live[0, 0, b, k].astype(BF16)
            part = dot(weight, rows)
            total = part if total is None else total + part
        aggregate[b * tile : (b + 1) * tile, :] = total


def add_border(total, received, tiles, block):
    grp, rot = lax.axis_index("grp"), lax.axis_index("rot")
    par_grp, par_rot = lax.rem(grp, 2), lax.rem(rot, 2)
    sides = (1 - par_grp, par_grp, 3 - par_rot, 2 + par_rot)
    size = tiles.shape[-2]
    for side, rows in zip(sides, received):
        index = jnp.where(side < 2, grp, rot)
        count = jnp.where(side < 2, lax.axis_size("grp"), lax.axis_size("rot"))
        above = lax.rem(side, 2) == 1
        inside = jnp.where(above, index + 1 < count, index > 0)
        part = dot(tiles[0, 0, pl.ds(side, 1)][0], rows[: tiles.shape[-1], :]) * inside.astype(F32)
        at = pl.ds(pl.multiple_of(block[0, 0, side] * size, size), size)
        total[at, :] += part


def middle_kernel(
    state, aggregate, rec0, rec1, rec2, rec3, tiles, block, w_msg, w_upd, chosen,
    state_out, messages_out, rim0, rim1, rim2, rim3, total,
):
    total[...] = aggregate[...]
    add_border(total, (rec0, rec1, rec2, rec3), tiles, block)
    new = state[...].astype(F32) + dot(gelu(total[...]).astype(BF16), w_upd[0])
    state_out[...] = new
    messages = dot(normed(new).astype(BF16), w_msg[1]).astype(BF16)
    messages_out[...] = messages
    make_rims(messages, chosen, (rim0, rim1, rim2, rim3))


def slot_of(peer, rank, me, members, capacity, light):
    away = lax.rem(peer - me - 1 + 2 * members, members)
    return jnp.where(away == 0, 0, capacity + light * (away - 1)) + rank


def ball_kernel(
    state, aggregate, rec0, rec1, rec2, rec3, tiles, block, w_upd, order, w_qkv,
    state_out, mixed, total,
):
    total[...] = aggregate[...]
    add_border(total, (rec0, rec1, rec2, rec3), tiles, block)
    points = state.shape[0]
    new = state[...] + dot(gelu(total[...]).astype(BF16), w_upd[1])
    state_out[...] = new
    unit = normed(new).astype(BF16)
    balled = [
        dot(picks(order[0][:, at : at + BALL], points), unit).astype(BF16)
        for at in range(0, points, BALL)
    ]

    def store(ball, value):
        mixed[ball * BALL : (ball + 1) * BALL, :] = value

    attention(jnp.concatenate(balled, axis=0), w_qkv[...], store)


def feed(pieces, w_in, w_mlp_out):
    inner = [dot(normed(piece).astype(BF16), w_in[...]) for piece in pieces]
    return [
        piece + dot(gelu(values).astype(BF16), w_mlp_out[...])
        for piece, values in zip(pieces, inner)
    ]


def sent_kernel(state, mixed, slots, w_out, w_in, w_mlp_out, *refs, start, after):
    outgoing = refs[after:]
    count = sum(out.shape[0] for out in outgoing)
    at_row = hot(iota((count, slots.shape[1]), 0) + start == slots[0:1, :])
    at_ball = hot(iota((count, slots.shape[1]), 0) + start == slots[1:2, :])
    back = dot(at_ball, mixed[...]).astype(BF16)
    rows = dot(at_row, state[...].astype(BF16))
    step = up_to(count // 2, 16)
    cuts = [slice(0, step), slice(step, count)]
    done = feed([rows[cut] + dot(back[cut], w_out[...]) for cut in cuts], w_in, w_mlp_out)
    units = jnp.concatenate([normed(piece).astype(BF16) for piece in done], axis=0)
    at = 0
    for out in outgoing:
        out[...] = units[at : at + out.shape[0]]
        at += out.shape[0]


def kept_kernel(state, mixed, order, w_out, after, state_out):
    back = dot(places(order[0], state.shape[0]), mixed[...]).astype(BF16)
    state_out[...] = state[...] + dot(back, w_out[...])


def owner_kernel(after, inbox, w_qkv, *refs, members, capacity, light, wide):
    incoming, returned = refs[:members], refs[members : 2 * members - 1]
    mixed, rows_in = refs[2 * members - 1 :]
    me = lax.axis_index("rot")
    points = mixed.shape[0]
    indices = []
    at = 0
    for away, rows in enumerate(incoming):
        height = rows.shape[0]
        span = capacity if away == 0 else wide
        sender = lax.rem(me - away + members, members)
        rows_in[at : at + height, :] = rows[...]
        if span > height:
            rows_in[at + height : at + span, :] = jnp.zeros((span - height, rows_in.shape[1]), BF16)
        indices.append(inbox[pl.ds(sender, 1), :][:, :span])
        at += span
    index_row = jnp.concatenate(indices, axis=1)
    owned = dot(places(index_row, points), rows_in[...]).astype(BF16)

    def store(ball, value):
        mixed[ball * BALL : (ball + 1) * BALL, :] = value

    attention(owned, w_qkv[...], store)
    for index, out in zip(indices[1:], returned):
        out[...] = dot(picks(index, points), mixed[...])[: out.shape[0]].astype(BF16)


def stayed_kernel(
    state, mixed, inbox, peer, rank, w_in, w_mlp_out, w_out, after, out,
    *, members, capacity, light,
):
    me = lax.axis_index("rot")
    back = dot(picks(inbox[pl.ds(me, 1), :], mixed.shape[0]), mixed[...]).astype(BF16)
    slots = slot_of(peer[0], rank[0], me, members, capacity, light)
    update = dot(picks(slots, capacity), back).astype(BF16)
    starts = range(0, state.shape[0], BALL)
    pieces = feed([state[at : at + BALL, :] for at in starts], w_in, w_mlp_out)
    for at, piece in zip(starts, pieces):
        out[at : at + BALL, :] = piece + dot(update[at : at + BALL], w_out[...])


def last_kernel(state, peer, rank, w_out, *refs, members, capacity, light, wide):
    returned, out, rows_in = refs[: members - 1], *refs[members - 1 :]
    me = lax.axis_index("rot")
    for at, rows in enumerate(returned):
        rows_in[at * wide : at * wide + light, :] = rows[...]
        if wide > light:
            rows_in[at * wide + light : (at + 1) * wide, :] = jnp.zeros(
                (wide - light, rows_in.shape[1]), BF16
            )
    slots = slot_of(peer[0], rank[0], me, members, capacity, wide) - capacity
    update = dot(picks(slots, rows_in.shape[0]), rows_in[...]).astype(BF16)
    out[...] = state[...] + dot(update, w_out[...])


VMEM = pl.BlockSpec(memory_space=pltpu.VMEM)
SMEM = pl.BlockSpec(memory_space=pltpu.SMEM)


def call(kernel, args, outs, scalars=(), scratch=(), flops=0, moved=1 << 20, name=None):
    return pl.pallas_call(
        kernel,
        out_shape=[jax.ShapeDtypeStruct(shape, kind) for shape, kind in outs],
        in_specs=[SMEM if i in scalars else VMEM for i in range(len(args))],
        out_specs=[VMEM] * len(outs),
        scratch_shapes=[pltpu.VMEM(shape, kind) for shape, kind in scratch],
        compiler_params=pltpu.CompilerParams(vmem_limit_bytes=48 * 1024 * 1024),
        cost_estimate=pl.CostEstimate(flops=flops, bytes_accessed=moved, transcendentals=0),
        name=name,
    )(*args)


def bound(kernel, **kw):
    return lambda *refs: kernel(*refs, **kw)


def swaps(axis, first):
    n_grp, n_rot = lax.axis_size("grp"), lax.axis_size("rot")
    count = n_grp if axis == "grp" else n_rot
    partner = {i: i for i in range(count)}
    for low in range(first, count - 1, 2):
        partner[low], partner[low + 1] = low + 1, low
    if axis == "rot" and first == 1 and count % 2 == 0:
        partner[0], partner[count - 1] = count - 1, 0
    out = []
    for g in range(n_grp):
        for r in range(n_rot):
            to = (partner[g], r) if axis == "grp" else (g, partner[r])
            if to == (g, r) and axis == "grp" and n_rot % 2 == 0:
                to = (g, r ^ 1)
            out.append((g * n_rot + r, to[0] * n_rot + to[1]))
    return out


def exchange(rims):
    plan = [swaps("grp", 0), swaps("grp", 1), swaps("rot", 0), swaps("rot", 1)]
    moved = [None] * 4
    for i in (1, 0, 3, 2):
        moved[i] = lax.ppermute(rims[i], ("grp", "rot"), plan[i])
    return moved


def relay(parts, members, back):
    moved = []
    for at, rows in enumerate(parts):
        step = members - 1 - at if back else at + 1
        turn = [(i, (i + step) % members) for i in range(members)]
        moved.append(lax.ppermute(rows, "rot", turn))
    return moved


def local(
    features, w_msg, w_upd, local_tiles, local_src, local_live, border_tiles, border_rows,
    border_block, ball_order, w_ball_qkv, w_ball_out, w_mlp_in, w_mlp_out, w_rot_qkv,
    w_rot_out, relay_peer, relay_rank, relay_inbox,
):
    points, width = features.shape
    members, capacity = lax.axis_size("rot"), relay_inbox.shape[-1]
    rim = border_rows.shape[-1]
    most = up_to(points - capacity, members - 1) // (members - 1)
    light, wide = up_to(most, 16), up_to(most, LANES)
    digits = 2 * members * (capacity // width)
    rims_shape = [((rim, width), BF16)] * 4
    first_shape = rims_shape[:2] + [((rim + digits, width), BF16)] * 2
    grid, grid16 = ((points, width), F32), ((points, width), BF16)

    (chosen,) = call(
        rim_kernel, (border_rows,), [((4, rim, LANES), jnp.int32)], flops=1 << 31,
        moved=1 << 23, name="rim_rows",
    )
    sizes = dict(members=members, capacity=capacity, light=light)
    part_shapes = [((capacity, width), BF16)] + [((light, width), BF16)] * (members - 1)

    messages, *rims = call(
        first_kernel, (chosen, features, w_msg, relay_inbox), [grid16] + first_shape,
        name="first_messages",
    )
    received = exchange(rims)
    (aggregate,) = call(
        local_kernel, (messages, local_tiles, local_src, local_live), [grid], scalars=(2, 3),
        name="local_edges",
    )
    state, messages, *rims = call(
        middle_kernel,
        (features, aggregate, *received, border_tiles, border_block, w_msg, w_upd, chosen),
        [grid, grid16] + rims_shape, scalars=(7,), scratch=[grid], name="second_messages",
    )
    slots, inbox = call(
        bound(slots_kernel, rim=rim, **sizes),
        (ball_order, relay_peer, relay_rank, received[2], received[3], messages),
        [((2, points), jnp.int32), ((members, capacity), jnp.int32)], name="slots",
    )
    received = exchange(rims)
    (aggregate,) = call(
        local_kernel, (messages, local_tiles, local_src, local_live), [grid], scalars=(2, 3),
        name="local_edges_again",
    )
    state, mixed = call(
        ball_kernel,
        (
            state, aggregate, *received, border_tiles, border_block, w_upd, ball_order,
            w_ball_qkv,
        ),
        [grid, grid16], scalars=(7,), scratch=[grid], name="ball_attention",
    )
    weights = (w_ball_out, w_mlp_in, w_mlp_out)
    parts = call(
        bound(sent_kernel, start=capacity, after=0), (state, mixed, slots, *weights),
        part_shapes[1:], name="light_rows",
    )
    heavy = call(
        bound(sent_kernel, start=0, after=1), (state, mixed, slots, *weights, parts[0]),
        part_shapes[:1], name="heavy_rows",
    )
    (state,) = call(
        kept_kernel, (state, mixed, ball_order, w_ball_out, heavy[0]), [grid], name="kept_rows"
    )
    parts = relay(parts, members, False)
    rows_in = ((capacity + (members - 1) * wide, width), BF16)
    *parts, mixed = call(
        bound(owner_kernel, wide=wide, **sizes), (state, inbox, w_rot_qkv, *heavy, *parts),
        part_shapes[1:] + [grid16], scratch=[rows_in], name="owner_layer",
    )
    (state,) = call(
        bound(stayed_kernel, **sizes),
        (
            state, mixed, inbox, relay_peer, relay_rank, w_mlp_in, w_mlp_out, w_rot_out, parts[0],
        ),
        [grid], name="stayed_changes",
    )
    parts = relay(parts, members, True)
    rows_in = (((members - 1) * wide, width), BF16)
    (out,) = call(
        bound(last_kernel, wide=wide, **sizes), (state, relay_peer, relay_rank, w_rot_out, *parts),
        [grid], scratch=[rows_in], name="relayed_changes",
    )
    return out


def solution(mesh):
    table = P("grp", "rot", None)
    in_specs = (
        P(("grp", "rot"), None), P(), P(),
        P("grp", "rot", None, None, None, None),
        P("grp", "rot", None, None), P("grp", "rot", None, None),
        P("grp", "rot", None, None, None),
        P("grp", "rot", None, None), table, table,
        P(), P(), P(), P(), P(), P(),
        table, table, P("grp", "rot", None, None),
    )
    out_specs = P(("grp", "rot"), None)
    return jax.shard_map(local, mesh=mesh, in_specs=in_specs, out_specs=out_specs, check_vma=False)
```

```python
import math

import jax
import jax.numpy as jnp
from jax import lax
from jax.experimental import pallas as pl
from jax.experimental.pallas import tpu as pltpu
from jax.sharding import PartitionSpec as P

HEADS = 8
BALL = 256
EPSILON = 1e-06
F32 = jnp.float32
BF16 = jnp.bfloat16
LANES = 128
DIGIT = 32


def up_to(count, unit):
    return -(-count // unit) * unit


def dot(left, right):
    return jnp.dot(left, right, preferred_element_type=F32)


def dot_rows(left, right):
    return lax.dot_general(left, right, (((1,), (1,)), ((), ())), preferred_element_type=F32)


def normed(values):
    return values * lax.rsqrt(jnp.mean(values * values, axis=-1, keepdims=True) + EPSILON)


def iota(shape, axis):
    return lax.broadcasted_iota(jnp.int32, shape, axis)


def hot(mask):
    return jnp.where(mask, 1.0, 0.0).astype(BF16)


def column(lane_row):
    return jnp.transpose(jnp.broadcast_to(lane_row, (LANES, LANES)))


def columns(lane_rows):
    count = lane_rows.shape[1]
    return jnp.concatenate([column(lane_rows[:, at : at + LANES]) for at in range(0, count, LANES)], axis=0)


def picks_by(cols, width):
    lane = iota(cols.shape, 1)
    return jnp.concatenate([hot(cols == lane + at) for at in range(0, width, LANES)], axis=1)


def picks(lane_rows, width):
    return picks_by(columns(lane_rows), width)


def places(lane_rows, height):
    return hot(iota((height, lane_rows.shape[1]), 0) == lane_rows)


def attention(rows_in, weight_qkv, store):
    width = rows_in.shape[1]
    head = width // HEADS
    scale = math.log2(math.e) / math.sqrt(head)
    lane_head = iota((1, width), 1) // head
    masks = [hot(lane_head == h) for h in range(HEADS)]
    joined = dot(rows_in, weight_qkv).astype(BF16)

    def mix(ball, weights, values):
        spread = jnp.concatenate([values * mask for mask in masks], axis=0)
        store(ball, dot(jnp.concatenate(weights, axis=1), spread).astype(BF16))

    pending = None
    for ball in range(rows_in.shape[0] // BALL):
        own = joined[ball * BALL : (ball + 1) * BALL]
        query, keys, values = own[:, :width], own[:, width : 2 * width], own[:, 2 * width :]
        weights = []
        for h in range(HEADS):
            near = slice(h * head // LANES * LANES, (h * head // LANES + 1) * LANES)
            scores = dot_rows(query[:, near] * masks[h][:, near], keys[:, near])
            top = jnp.max(scores, axis=-1, keepdims=True)
            raw = jnp.exp2((scores - top) * scale)
            weights.append((raw * (1.0 / jnp.sum(raw, axis=-1, keepdims=True))).astype(BF16))
        if pending is not None:
            mix(*pending)
        pending = (ball, weights, values)
    mix(*pending)


def gelu(values):
    root = math.sqrt(2.0 / math.pi)
    inner = values * (root + (root * 0.044715) * (values * values))
    return values * (0.5 + 0.5 * jnp.tanh(inner))


def rim_kernel(rim_rows, chosen):
    par_grp, par_rot = lax.rem(lax.axis_index("grp"), 2), lax.rem(lax.axis_index("rot"), 2)
    for at, side in enumerate((1 - par_grp, par_grp, 3 - par_rot, 2 + par_rot)):
        chosen[at] = columns(rim_rows[0, 0, pl.ds(side, 1), :])


def make_rims(messages, chosen, out_refs):
    for at, out in enumerate(out_refs):
        out[: chosen.shape[1], :] = dot(picks_by(chosen[at], messages.shape[0]), messages).astype(BF16)


def first_kernel(chosen, features, w_msg, inbox, messages_out, *rims_out):
    points, width = features.shape
    messages = [
        dot(normed(features[at : at + BALL, :].astype(F32)).astype(BF16), w_msg[0]).astype(BF16)
        for at in range(0, points, BALL)
    ]
    messages = jnp.concatenate(messages, axis=0)
    messages_out[...] = messages
    make_rims(messages, chosen, rims_out)
    table = inbox[0, 0]
    pieces = [table[:, at : at + width] for at in range(0, table.shape[1], width)]
    digits = [piece // DIGIT for piece in pieces] + [lax.rem(piece, DIGIT) for piece in pieces]
    digits = jnp.concatenate(digits, axis=0).astype(F32).astype(BF16)
    for out in rims_out:
        out[chosen.shape[1] :, :] = digits


def slots_kernel(
    order, peer, rank, rec2, rec3, after, slots_out, inbox_out, *, members, capacity, light, rim
):
    me = lax.axis_index("rot")
    slots = slot_of(peer[0], rank[0], me, members, capacity, light)
    points = slots.shape[1]
    digits = jnp.concatenate([slots // LANES, lax.rem(slots, LANES)] + [jnp.zeros_like(slots)] * 6, axis=0)
    moved = dot(digits.astype(F32).astype(BF16), places(order[0], points)).astype(jnp.int32)
    slots_out[0:1, :] = slots
    slots_out[1:2, :] = moved[0:1] * LANES + moved[1:2]
    even = (lax.rem(me, 2) == 0).astype(F32)
    table = rec2[rim:, :].astype(F32) * even + rec3[rim:, :].astype(F32) * (1.0 - even)
    half = table.shape[0] // 2
    table = (table[:half] * DIGIT + table[half:]).astype(jnp.int32)
    width = table.shape[1]
    for at in range(0, capacity, width):
        first = at // width * members
        inbox_out[:, at : at + width] = table[first : first + members]


def local_kernel(messages, tiles, source, live, aggregate):
    tile = tiles.shape[-1]
    blocks, sources = tiles.shape[2], tiles.shape[3]
    for b in range(blocks):
        total = None
        for k in range(sources):
            rows = messages[pl.ds(pl.multiple_of(source[0, 0, b, k] * tile, tile), tile), :]
            weight = tiles[0, 0, b, k] * live[0, 0, b, k].astype(BF16)
            part = dot(weight, rows)
            total = part if total is None else total + part
        aggregate[b * tile : (b + 1) * tile, :] = total


def add_border(total, received, tiles, block):
    grp, rot = lax.axis_index("grp"), lax.axis_index("rot")
    par_grp, par_rot = lax.rem(grp, 2), lax.rem(rot, 2)
    sides = (1 - par_grp, par_grp, 3 - par_rot, 2 + par_rot)
    size = tiles.shape[-2]
    for side, rows in zip(sides, received):
        index = jnp.where(side < 2, grp, rot)
        count = jnp.where(side < 2, lax.axis_size("grp"), lax.axis_size("rot"))
        above = lax.rem(side, 2) == 1
        inside = jnp.where(above, index + 1 < count, index > 0)
        part = dot(tiles[0, 0, pl.ds(side, 1)][0], rows[: tiles.shape[-1], :]) * inside.astype(F32)
        at = pl.ds(pl.multiple_of(block[0, 0, side] * size, size), size)
        total[at, :] += part


def middle_kernel(
    state, aggregate, rec0, rec1, rec2, rec3, tiles, block, w_msg, w_upd, chosen,
    state_out, messages_out, rim0, rim1, rim2, rim3, total,
):
    total[...] = aggregate[...]
    add_border(total, (rec0, rec1, rec2, rec3), tiles, block)
    new = state[...].astype(F32) + dot(gelu(total[...]).astype(BF16), w_upd[0])
    state_out[...] = new
    messages = dot(normed(new).astype(BF16), w_msg[1]).astype(BF16)
    messages_out[...] = messages
    make_rims(messages, chosen, (rim0, rim1, rim2, rim3))


def partner(me, step, members):
    return me ^ step if members & (members - 1) == 0 else (me + step) % members


def slot_of(peer, rank, me, members, capacity, light):
    worker = lax.rem(peer - 1 + members, members)
    away = me ^ worker if members & (members - 1) == 0 else lax.rem(worker - me + members, members)
    return jnp.where(away == 0, 0, capacity + light * (away - 1)) + rank


def ball_kernel(
    state, aggregate, rec0, rec1, rec2, rec3, tiles, block, w_upd, order, w_qkv,
    state_out, mixed, total,
):
    total[...] = aggregate[...]
    add_border(total, (rec0, rec1, rec2, rec3), tiles, block)
    points = state.shape[0]
    new = state[...] + dot(gelu(total[...]).astype(BF16), w_upd[1])
    state_out[...] = new
    unit = normed(new).astype(BF16)
    balled = [
        dot(picks(order[0][:, at : at + BALL], points), unit).astype(BF16)
        for at in range(0, points, BALL)
    ]

    def store(ball, value):
        mixed[ball * BALL : (ball + 1) * BALL, :] = value

    attention(jnp.concatenate(balled, axis=0), w_qkv[...], store)


def feed(pieces, w_in, w_mlp_out):
    inner = [dot(normed(piece).astype(BF16), w_in[...]) for piece in pieces]
    return [
        piece + dot(gelu(values).astype(BF16), w_mlp_out[...])
        for piece, values in zip(pieces, inner)
    ]


def sent_kernel(state, mixed, slots, w_out, w_in, w_mlp_out, *refs, start, after):
    outgoing = refs[after:]
    count = sum(out.shape[0] for out in outgoing)
    at_row = hot(iota((count, slots.shape[1]), 0) + start == slots[0:1, :])
    at_ball = hot(iota((count, slots.shape[1]), 0) + start == slots[1:2, :])
    back = dot(at_ball, mixed[...]).astype(BF16)
    rows = dot(at_row, state[...].astype(BF16))
    step = up_to(count // 2, 16)
    cuts = [slice(0, step), slice(step, count)]
    done = feed([rows[cut] + dot(back[cut], w_out[...]) for cut in cuts], w_in, w_mlp_out)
    units = jnp.concatenate([normed(piece).astype(BF16) for piece in done], axis=0)
    at = 0
    for out in outgoing:
        out[...] = units[at : at + out.shape[0]]
        at += out.shape[0]


def kept_kernel(state, mixed, order, w_out, after, state_out):
    back = dot(places(order[0], state.shape[0]), mixed[...]).astype(BF16)
    state_out[...] = state[...] + dot(back, w_out[...])


def owner_kernel(after, inbox, w_qkv, *refs, members, capacity, light, wide):
    incoming, returned = refs[:members], refs[members : 2 * members - 1]
    mixed, rows_in = refs[2 * members - 1 :]
    me = lax.axis_index("rot")
    points = mixed.shape[0]
    indices = []
    at = 0
    for away, rows in enumerate(incoming):
        height = rows.shape[0]
        span = capacity if away == 0 else wide
        sender = partner(me, away if members & (members - 1) == 0 else members - away, members)
        rows_in[at : at + height, :] = rows[...]
        if span > height:
            rows_in[at + height : at + span, :] = jnp.zeros((span - height, rows_in.shape[1]), BF16)
        indices.append(inbox[pl.ds(sender, 1), :][:, :span])
        at += span
    index_row = jnp.concatenate(indices, axis=1)
    owned = dot(places(index_row, points), rows_in[...]).astype(BF16)

    def store(ball, value):
        mixed[ball * BALL : (ball + 1) * BALL, :] = value

    attention(owned, w_qkv[...], store)
    chosen = jnp.concatenate([picks(index, points)[:light] for index in indices[1:]], axis=0)
    back = dot(chosen, mixed[...]).astype(BF16)
    for at, out in enumerate(returned):
        out[...] = back[at * light : (at + 1) * light]


def stayed_kernel(
    state, mixed, inbox, peer, rank, w_in, w_mlp_out, w_out, after, out,
    *, members, capacity, light,
):
    me = lax.axis_index("rot")
    back = dot(picks(inbox[pl.ds(me, 1), :], mixed.shape[0]), mixed[...]).astype(BF16)
    slots = slot_of(peer[0], rank[0], me, members, capacity, light)
    update = dot(picks(slots, capacity), back).astype(BF16)
    starts = range(0, state.shape[0], BALL)
    pieces = feed([state[at : at + BALL, :] for at in starts], w_in, w_mlp_out)
    for at, piece in zip(starts, pieces):
        out[at : at + BALL, :] = piece + dot(update[at : at + BALL], w_out[...])


def last_kernel(state, peer, rank, w_out, *refs, members, capacity, light, wide):
    returned, out, rows_in = refs[: members - 1], *refs[members - 1 :]
    me = lax.axis_index("rot")
    for at, rows in enumerate(returned):
        rows_in[at * wide : at * wide + light, :] = rows[...]
        if wide > light:
            rows_in[at * wide + light : (at + 1) * wide, :] = jnp.zeros(
                (wide - light, rows_in.shape[1]), BF16
            )
    slots = slot_of(peer[0], rank[0], me, members, capacity, wide) - capacity
    update = dot(picks(slots, rows_in.shape[0]), rows_in[...]).astype(BF16)
    out[...] = state[...] + dot(update, w_out[...])


VMEM = pl.BlockSpec(memory_space=pltpu.VMEM)
SMEM = pl.BlockSpec(memory_space=pltpu.SMEM)


def call(kernel, args, outs, scalars=(), scratch=(), flops=0, moved=1 << 20, name=None):
    return pl.pallas_call(
        kernel,
        out_shape=[jax.ShapeDtypeStruct(shape, kind) for shape, kind in outs],
        in_specs=[SMEM if i in scalars else VMEM for i in range(len(args))],
        out_specs=[VMEM] * len(outs),
        scratch_shapes=[pltpu.VMEM(shape, kind) for shape, kind in scratch],
        compiler_params=pltpu.CompilerParams(vmem_limit_bytes=48 * 1024 * 1024),
        cost_estimate=pl.CostEstimate(flops=flops, bytes_accessed=moved, transcendentals=0),
        name=name,
    )(*args)


def bound(kernel, **kw):
    return lambda *refs: kernel(*refs, **kw)


def swaps(axis, first):
    n_grp, n_rot = lax.axis_size("grp"), lax.axis_size("rot")
    count = n_grp if axis == "grp" else n_rot
    partner = {i: i for i in range(count)}
    for low in range(first, count - 1, 2):
        partner[low], partner[low + 1] = low + 1, low
    if axis == "rot" and first == 1 and count % 2 == 0:
        partner[0], partner[count - 1] = count - 1, 0
    out = []
    for g in range(n_grp):
        for r in range(n_rot):
            to = (partner[g], r) if axis == "grp" else (g, partner[r])
            if to == (g, r) and axis == "grp" and n_rot % 2 == 0:
                to = (g, r ^ 1)
            out.append((g * n_rot + r, to[0] * n_rot + to[1]))
    return out


def exchange(rims):
    plan = [swaps("grp", 0), swaps("grp", 1), swaps("rot", 0), swaps("rot", 1)]
    moved = [None] * 4
    for i in (1, 0, 3, 2):
        moved[i] = lax.ppermute(rims[i], ("grp", "rot"), plan[i])
    return moved


def relay(parts, members, back):
    moved = []
    for at, rows in enumerate(parts):
        pairs = [(i, int(partner(i, at + 1, members))) for i in range(members)]
        moved.append(lax.ppermute(rows, "rot", [pair[::-1] for pair in pairs] if back else pairs))
    return moved


def local(
    features, w_msg, w_upd, local_tiles, local_src, local_live, border_tiles, border_rows,
    border_block, ball_order, w_ball_qkv, w_ball_out, w_mlp_in, w_mlp_out, w_rot_qkv,
    w_rot_out, relay_peer, relay_rank, relay_inbox,
):
    points, width = features.shape
    members, capacity = lax.axis_size("rot"), relay_inbox.shape[-1]
    rim = border_rows.shape[-1]
    most = up_to(points - capacity, members - 1) // (members - 1)
    light, wide = up_to(most, 16), up_to(most, LANES)
    digits = 2 * members * (capacity // width)
    rims_shape = [((rim, width), BF16)] * 4
    first_shape = [((rim + digits, width), BF16)] * 4
    grid, grid16 = ((points, width), F32), ((points, width), BF16)

    (chosen,) = call(
        rim_kernel, (border_rows,), [((4, rim, LANES), jnp.int32)], flops=1 << 31,
        moved=1 << 23, name="rim_rows",
    )
    sizes = dict(members=members, capacity=capacity, light=light)
    part_shapes = [((capacity, width), BF16)] + [((light, width), BF16)] * (members - 1)

    messages, *rims = call(
        first_kernel, (chosen, features, w_msg, relay_inbox), [grid16] + first_shape,
        name="first_messages",
    )
    received = exchange(rims)
    (aggregate,) = call(
        local_kernel, (messages, local_tiles, local_src, local_live), [grid], scalars=(2, 3),
        name="local_edges",
    )
    state, messages, *rims = call(
        middle_kernel,
        (features, aggregate, *received, border_tiles, border_block, w_msg, w_upd, chosen),
        [grid, grid16] + rims_shape, scalars=(7,), scratch=[grid], name="second_messages",
    )
    slots, inbox = call(
        bound(slots_kernel, rim=rim, **sizes),
        (ball_order, relay_peer, relay_rank, received[2], received[3], messages),
        [((2, points), jnp.int32), ((members, capacity), jnp.int32)], name="slots",
    )
    received = exchange(rims)
    (aggregate,) = call(
        local_kernel, (messages, local_tiles, local_src, local_live), [grid], scalars=(2, 3),
        name="local_edges_again",
    )
    state, mixed = call(
        ball_kernel,
        (
            state, aggregate, *received, border_tiles, border_block, w_upd, ball_order,
            w_ball_qkv,
        ),
        [grid, grid16], scalars=(7,), scratch=[grid], name="ball_attention",
    )
    weights = (w_ball_out, w_mlp_in, w_mlp_out)
    parts = call(
        bound(sent_kernel, start=capacity, after=0), (state, mixed, slots, *weights),
        part_shapes[1:], name="light_rows",
    )
    heavy = call(
        bound(sent_kernel, start=0, after=1), (state, mixed, slots, *weights, parts[0]),
        part_shapes[:1], name="heavy_rows",
    )
    (state,) = call(
        kept_kernel, (state, mixed, ball_order, w_ball_out, heavy[0]), [grid], name="kept_rows"
    )
    parts = relay(parts, members, False)
    rows_in = ((capacity + (members - 1) * wide, width), BF16)
    *parts, mixed = call(
        bound(owner_kernel, wide=wide, **sizes), (state, inbox, w_rot_qkv, *heavy, *parts),
        part_shapes[1:] + [grid16], scratch=[rows_in], name="owner_layer",
    )
    (state,) = call(
        bound(stayed_kernel, **sizes),
        (
            state, mixed, inbox, relay_peer, relay_rank, w_mlp_in, w_mlp_out, w_rot_out, parts[0],
        ),
        [grid], name="stayed_changes",
    )
    parts = relay(parts, members, True)
    rows_in = (((members - 1) * wide, width), BF16)
    (out,) = call(
        bound(last_kernel, wide=wide, **sizes), (state, relay_peer, relay_rank, w_rot_out, *parts),
        [grid], scratch=[rows_in], name="relayed_changes",
    )
    return out


def solution(mesh):
    table = P("grp", "rot", None)
    in_specs = (
        P(("grp", "rot"), None), P(), P(),
        P("grp", "rot", None, None, None, None),
        P("grp", "rot", None, None), P("grp", "rot", None, None),
        P("grp", "rot", None, None, None),
        P("grp", "rot", None, None), table, table,
        P(), P(), P(), P(), P(), P(),
        table, table, P("grp", "rot", None, None),
    )
    out_specs = P(("grp", "rot"), None)
    return jax.shard_map(local, mesh=mesh, in_specs=in_specs, out_specs=out_specs, check_vma=False)
```

```python
import math

import jax
import jax.numpy as jnp
from jax import lax
from jax.experimental import pallas as pl
from jax.experimental.pallas import tpu as pltpu
from jax.sharding import PartitionSpec as P

HEADS = 8
BALL = 256
EPSILON = 1e-06
F32 = jnp.float32
BF16 = jnp.bfloat16
LANES = 128
DIGIT = 32


def up_to(count, unit):
    return -(-count // unit) * unit


def dot(left, right):
    return jnp.dot(left, right, preferred_element_type=F32)


def dot_rows(left, right):
    return lax.dot_general(left, right, (((1,), (1,)), ((), ())), preferred_element_type=F32)


def normed(values):
    return values * lax.rsqrt(jnp.mean(values * values, axis=-1, keepdims=True) + EPSILON)


def iota(shape, axis):
    return lax.broadcasted_iota(jnp.int32, shape, axis)


def hot(mask):
    return jnp.where(mask, 1.0, 0.0).astype(BF16)


def column(lane_row):
    return jnp.transpose(jnp.broadcast_to(lane_row, (LANES, LANES)))


def columns(lane_rows):
    count = lane_rows.shape[1]
    return jnp.concatenate([column(lane_rows[:, at : at + LANES]) for at in range(0, count, LANES)], axis=0)


def picks_by(cols, width):
    lane = iota(cols.shape, 1)
    return jnp.concatenate([hot(cols == lane + at) for at in range(0, width, LANES)], axis=1)


def picks(lane_rows, width):
    return picks_by(columns(lane_rows), width)


def places(lane_rows, height):
    return hot(iota((height, lane_rows.shape[1]), 0) == lane_rows)


def attention(rows_in, weight_qkv, store, late=False):
    width = rows_in.shape[1]
    head = width // HEADS
    scale = math.log2(math.e) / math.sqrt(head)
    lane_head = iota((1, width), 1) // head
    masks = [hot(lane_head == h) for h in range(HEADS)]
    joined = dot(rows_in, weight_qkv).astype(BF16)

    def mix(ball, weights, scales, values):
        spread = jnp.concatenate([values * mask for mask in masks], axis=0)
        mixed = dot(jnp.concatenate(weights, axis=1), spread)
        if late:
            scale_of = jnp.broadcast_to(scales[0], mixed.shape)
            for h in range(1, HEADS):
                scale_of = jnp.where(lane_head == h, scales[h], scale_of)
            mixed = mixed * scale_of
        store(ball, mixed.astype(BF16))

    pending = None
    for ball in range(rows_in.shape[0] // BALL):
        own = joined[ball * BALL : (ball + 1) * BALL]
        query, keys, values = own[:, :width], own[:, width : 2 * width], own[:, 2 * width :]
        weights, scales = [], []
        for h in range(HEADS):
            near = slice(h * head // LANES * LANES, (h * head // LANES + 1) * LANES)
            scores = dot_rows(query[:, near] * masks[h][:, near], keys[:, near])
            top = jnp.max(scores, axis=-1, keepdims=True)
            raw = jnp.exp2((scores - top) * scale)
            scales.append(1.0 / jnp.sum(raw, axis=-1, keepdims=True))
            weights.append((raw if late else raw * scales[-1]).astype(BF16))
        if pending is not None:
            mix(*pending)
        pending = (ball, weights, scales, values)
    mix(*pending)


def gelu(values):
    root = math.sqrt(2.0 / math.pi)
    inner = values * (root + (root * 0.044715) * (values * values))
    return values * (0.5 + 0.5 * jnp.tanh(inner))


def rim_kernel(rim_rows, chosen):
    par_grp, par_rot = lax.rem(lax.axis_index("grp"), 2), lax.rem(lax.axis_index("rot"), 2)
    for at, side in enumerate((1 - par_grp, par_grp, 3 - par_rot, 2 + par_rot)):
        chosen[at] = columns(rim_rows[0, 0, pl.ds(side, 1), :])


def make_rims(messages, chosen, out_refs):
    for at, out in enumerate(out_refs):
        out[: chosen.shape[1], :] = dot(picks_by(chosen[at], messages.shape[0]), messages).astype(BF16)


def first_kernel(chosen, features, w_msg, inbox, messages_out, *rims_out):
    points, width = features.shape
    messages = [
        dot(normed(features[at : at + BALL, :].astype(F32)).astype(BF16), w_msg[0]).astype(BF16)
        for at in range(0, points, BALL)
    ]
    messages = jnp.concatenate(messages, axis=0)
    messages_out[...] = messages
    make_rims(messages, chosen, rims_out)
    table = inbox[0, 0]
    pieces = [table[:, at : at + width] for at in range(0, table.shape[1], width)]
    digits = [piece // DIGIT for piece in pieces] + [lax.rem(piece, DIGIT) for piece in pieces]
    digits = jnp.concatenate(digits, axis=0).astype(F32).astype(BF16)
    for out in rims_out:
        out[chosen.shape[1] :, :] = digits


def slots_kernel(
    order, peer, rank, rec2, rec3, after, slots_out, inbox_out, *, members, capacity, light, rim
):
    me = lax.axis_index("rot")
    slots = slot_of(peer[0], rank[0], me, members, capacity, light)
    points = slots.shape[1]
    digits = jnp.concatenate([slots // LANES, lax.rem(slots, LANES)] + [jnp.zeros_like(slots)] * 6, axis=0)
    moved = dot(digits.astype(F32).astype(BF16), places(order[0], points)).astype(jnp.int32)
    slots_out[0:1, :] = slots
    slots_out[1:2, :] = moved[0:1] * LANES + moved[1:2]
    even = (lax.rem(me, 2) == 0).astype(F32)
    table = rec2[rim:, :].astype(F32) * even + rec3[rim:, :].astype(F32) * (1.0 - even)
    half = table.shape[0] // 2
    table = (table[:half] * DIGIT + table[half:]).astype(jnp.int32)
    width = table.shape[1]
    for at in range(0, capacity, width):
        first = at // width * members
        inbox_out[:, at : at + width] = table[first : first + members]


def local_kernel(messages, tiles, source, live, aggregate):
    tile = tiles.shape[-1]
    blocks, sources = tiles.shape[2], tiles.shape[3]
    for b in range(blocks):
        total = None
        for k in range(sources):
            rows = messages[pl.ds(pl.multiple_of(source[0, 0, b, k] * tile, tile), tile), :]
            weight = tiles[0, 0, b, k] * live[0, 0, b, k].astype(BF16)
            part = dot(weight, rows)
            total = part if total is None else total + part
        aggregate[b * tile : (b + 1) * tile, :] = total


def add_border(total, received, tiles, block):
    grp, rot = lax.axis_index("grp"), lax.axis_index("rot")
    par_grp, par_rot = lax.rem(grp, 2), lax.rem(rot, 2)
    sides = (1 - par_grp, par_grp, 3 - par_rot, 2 + par_rot)
    size = tiles.shape[-2]
    for side, rows in zip(sides, received):
        index = jnp.where(side < 2, grp, rot)
        count = jnp.where(side < 2, lax.axis_size("grp"), lax.axis_size("rot"))
        above = lax.rem(side, 2) == 1
        inside = jnp.where(above, index + 1 < count, index > 0)
        part = dot(tiles[0, 0, pl.ds(side, 1)][0], rows[: tiles.shape[-1], :]) * inside.astype(F32)
        at = pl.ds(pl.multiple_of(block[0, 0, side] * size, size), size)
        total[at, :] += part


def middle_kernel(
    state, aggregate, rec0, rec1, rec2, rec3, tiles, block, w_msg, w_upd, chosen,
    state_out, messages_out, rim0, rim1, rim2, rim3, total,
):
    total[...] = aggregate[...]
    add_border(total, (rec0, rec1, rec2, rec3), tiles, block)
    new = state[...].astype(F32) + dot(gelu(total[...]).astype(BF16), w_upd[0])
    state_out[...] = new
    messages = dot(normed(new).astype(BF16), w_msg[1]).astype(BF16)
    messages_out[...] = messages
    make_rims(messages, chosen, (rim0, rim1, rim2, rim3))


def partner(me, step, members):
    return me ^ step if members & (members - 1) == 0 else (me + step) % members


def slot_of(peer, rank, me, members, capacity, light):
    worker = lax.rem(peer - 1 + members, members)
    away = me ^ worker if members & (members - 1) == 0 else lax.rem(worker - me + members, members)
    return jnp.where(away == 0, 0, capacity + light * (away - 1)) + rank


def ball_kernel(
    state, aggregate, rec0, rec1, rec2, rec3, tiles, block, w_upd, order, w_qkv,
    state_out, mixed, total,
):
    total[...] = aggregate[...]
    add_border(total, (rec0, rec1, rec2, rec3), tiles, block)
    points = state.shape[0]
    new = state[...] + dot(gelu(total[...]).astype(BF16), w_upd[1])
    state_out[...] = new
    unit = normed(new).astype(BF16)
    balled = [
        dot(picks(order[0][:, at : at + BALL], points), unit).astype(BF16)
        for at in range(0, points, BALL)
    ]

    def store(ball, value):
        mixed[ball * BALL : (ball + 1) * BALL, :] = value

    attention(jnp.concatenate(balled, axis=0), w_qkv[...], store, late=True)


def feed(pieces, w_in, w_mlp_out):
    inner = [dot(normed(piece).astype(BF16), w_in[...]) for piece in pieces]
    return [
        piece + dot(gelu(values).astype(BF16), w_mlp_out[...])
        for piece, values in zip(pieces, inner)
    ]


def sent_kernel(state, mixed, slots, w_out, w_in, w_mlp_out, *refs, start, after):
    outgoing = refs[after:]
    count = sum(out.shape[0] for out in outgoing)
    at_row = hot(iota((count, slots.shape[1]), 0) + start == slots[0:1, :])
    at_ball = hot(iota((count, slots.shape[1]), 0) + start == slots[1:2, :])
    back = dot(at_ball, mixed[...]).astype(BF16)
    rows = dot(at_row, state[...].astype(BF16))
    step = up_to(count // 2, 16)
    cuts = [slice(0, step), slice(step, count)]
    done = feed([rows[cut] + dot(back[cut], w_out[...]) for cut in cuts], w_in, w_mlp_out)
    units = jnp.concatenate([normed(piece).astype(BF16) for piece in done], axis=0)
    at = 0
    for out in outgoing:
        out[...] = units[at : at + out.shape[0]]
        at += out.shape[0]


def kept_kernel(state, mixed, order, w_out, after, state_out):
    back = dot(places(order[0], state.shape[0]), mixed[...]).astype(BF16)
    state_out[...] = state[...] + dot(back, w_out[...])


def owner_kernel(after, inbox, w_qkv, *refs, members, capacity, light, wide):
    incoming, returned = refs[:members], refs[members : 2 * members - 1]
    mixed, rows_in = refs[2 * members - 1 :]
    me = lax.axis_index("rot")
    points = mixed.shape[0]
    indices = []
    at = 0
    for away, rows in enumerate(incoming):
        height = rows.shape[0]
        span = capacity if away == 0 else wide
        sender = partner(me, away if members & (members - 1) == 0 else members - away, members)
        rows_in[at : at + height, :] = rows[...]
        if span > height:
            rows_in[at + height : at + span, :] = jnp.zeros((span - height, rows_in.shape[1]), BF16)
        indices.append(inbox[pl.ds(sender, 1), :][:, :span])
        at += span
    index_row = jnp.concatenate(indices, axis=1)
    owned = dot(places(index_row, points), rows_in[...]).astype(BF16)

    def store(ball, value):
        mixed[ball * BALL : (ball + 1) * BALL, :] = value

    attention(owned, w_qkv[...], store)
    chosen = jnp.concatenate([picks(index, points)[:light] for index in indices[1:]], axis=0)
    back = dot(chosen, mixed[...]).astype(BF16)
    for at, out in enumerate(returned):
        out[...] = back[at * light : (at + 1) * light]


def stayed_kernel(
    state, mixed, inbox, peer, rank, w_in, w_mlp_out, w_out, after, out,
    *, members, capacity, light,
):
    me = lax.axis_index("rot")
    back = dot(picks(inbox[pl.ds(me, 1), :], mixed.shape[0]), mixed[...]).astype(BF16)
    slots = slot_of(peer[0], rank[0], me, members, capacity, light)
    update = dot(picks(slots, capacity), back).astype(BF16)
    starts = range(0, state.shape[0], BALL)
    pieces = feed([state[at : at + BALL, :] for at in starts], w_in, w_mlp_out)
    for at, piece in zip(starts, pieces):
        out[at : at + BALL, :] = piece + dot(update[at : at + BALL], w_out[...])


def last_kernel(state, peer, rank, w_out, *refs, members, capacity, light, wide):
    returned, out, rows_in, new, sems = refs[: members - 1], *refs[members - 1 :]
    me = lax.axis_index("rot")
    for at, rows in enumerate(returned):
        rows_in[at * wide : at * wide + light, :] = rows[...]
        if wide > light:
            rows_in[at * wide + light : (at + 1) * wide, :] = jnp.zeros(
                (wide - light, rows_in.shape[1]), BF16
            )
    slots = slot_of(peer[0], rank[0], me, members, capacity, wide) - capacity
    change = dot(rows_in[...], w_out[...]).astype(BF16)
    update = dot(picks(slots, rows_in.shape[0]), change)
    step = state.shape[0] // 4
    copies = []
    for c in range(4):
        rows = slice(c * step, (c + 1) * step)
        new[rows, :] = state[rows, :] + update[rows]
        copies.append(pltpu.make_async_copy(new.at[rows], out.at[rows], sems.at[c]))
        copies[-1].start()
    for copy in copies:
        copy.wait()


VMEM = pl.BlockSpec(memory_space=pltpu.VMEM)
SMEM = pl.BlockSpec(memory_space=pltpu.SMEM)


def call(kernel, args, outs, scalars=(), far_outs=(), scratch=(), sems=0, flops=0, moved=1 << 20, name=None):
    return pl.pallas_call(
        kernel,
        out_shape=[jax.ShapeDtypeStruct(shape, kind) for shape, kind in outs],
        in_specs=[SMEM if i in scalars else VMEM for i in range(len(args))],
        out_specs=[pl.BlockSpec(memory_space=pl.ANY) if i in far_outs else VMEM for i in range(len(outs))],
        scratch_shapes=[pltpu.VMEM(shape, kind) for shape, kind in scratch]
        + ([pltpu.SemaphoreType.DMA((sems,))] if sems else []),
        compiler_params=pltpu.CompilerParams(vmem_limit_bytes=48 * 1024 * 1024),
        cost_estimate=pl.CostEstimate(flops=flops, bytes_accessed=moved, transcendentals=0),
        name=name,
    )(*args)


def bound(kernel, **kw):
    return lambda *refs: kernel(*refs, **kw)


def swaps(axis, first):
    n_grp, n_rot = lax.axis_size("grp"), lax.axis_size("rot")
    count = n_grp if axis == "grp" else n_rot
    partner = {i: i for i in range(count)}
    for low in range(first, count - 1, 2):
        partner[low], partner[low + 1] = low + 1, low
    if axis == "rot" and first == 1 and count % 2 == 0:
        partner[0], partner[count - 1] = count - 1, 0
    out = []
    for g in range(n_grp):
        for r in range(n_rot):
            to = (partner[g], r) if axis == "grp" else (g, partner[r])
            if to == (g, r) and axis == "grp" and n_rot % 2 == 0:
                to = (g, r ^ 1)
            out.append((g * n_rot + r, to[0] * n_rot + to[1]))
    return out


def exchange(rims):
    plan = [swaps("grp", 0), swaps("grp", 1), swaps("rot", 0), swaps("rot", 1)]
    moved = [None] * 4
    for i in (1, 0, 3, 2):
        moved[i] = lax.ppermute(rims[i], ("grp", "rot"), plan[i])
    return moved


def relay(parts, members, back):
    moved = []
    for at, rows in enumerate(parts):
        pairs = [(i, int(partner(i, at + 1, members))) for i in range(members)]
        moved.append(lax.ppermute(rows, "rot", [pair[::-1] for pair in pairs] if back else pairs))
    return moved


def local(
    features, w_msg, w_upd, local_tiles, local_src, local_live, border_tiles, border_rows,
    border_block, ball_order, w_ball_qkv, w_ball_out, w_mlp_in, w_mlp_out, w_rot_qkv,
    w_rot_out, relay_peer, relay_rank, relay_inbox,
):
    points, width = features.shape
    members, capacity = lax.axis_size("rot"), relay_inbox.shape[-1]
    rim = border_rows.shape[-1]
    most = up_to(points - capacity, members - 1) // (members - 1)
    light, wide = up_to(most, 16), up_to(most, LANES)
    digits = 2 * members * (capacity // width)
    rims_shape = [((rim, width), BF16)] * 4
    first_shape = [((rim + digits, width), BF16)] * 4
    grid, grid16 = ((points, width), F32), ((points, width), BF16)

    (chosen,) = call(
        rim_kernel, (border_rows,), [((4, rim, LANES), jnp.int32)], flops=1 << 31,
        moved=1 << 23, name="rim_rows",
    )
    sizes = dict(members=members, capacity=capacity, light=light)
    part_shapes = [((capacity, width), BF16)] + [((light, width), BF16)] * (members - 1)

    messages, *rims = call(
        first_kernel, (chosen, features, w_msg, relay_inbox), [grid16] + first_shape,
        name="first_messages",
    )
    received = exchange(rims)
    (aggregate,) = call(
        local_kernel, (messages, local_tiles, local_src, local_live), [grid], scalars=(2, 3),
        name="local_edges",
    )
    state, messages, *rims = call(
        middle_kernel,
        (features, aggregate, *received, border_tiles, border_block, w_msg, w_upd, chosen),
        [grid, grid16] + rims_shape, scalars=(7,), scratch=[grid], name="second_messages",
    )
    slots, inbox = call(
        bound(slots_kernel, rim=rim, **sizes),
        (ball_order, relay_peer, relay_rank, received[2], received[3], messages),
        [((2, points), jnp.int32), ((members, capacity), jnp.int32)], name="slots",
    )
    received = exchange(rims)
    (aggregate,) = call(
        local_kernel, (messages, local_tiles, local_src, local_live), [grid], scalars=(2, 3),
        name="local_edges_again",
    )
    state, mixed = call(
        ball_kernel,
        (
            state, aggregate, *received, border_tiles, border_block, w_upd, ball_order,
            w_ball_qkv,
        ),
        [grid, grid16], scalars=(7,), scratch=[grid], name="ball_attention",
    )
    weights = (w_ball_out, w_mlp_in, w_mlp_out)
    parts = call(
        bound(sent_kernel, start=capacity, after=0), (state, mixed, slots, *weights),
        part_shapes[1:], name="light_rows",
    )
    heavy = call(
        bound(sent_kernel, start=0, after=1), (state, mixed, slots, *weights, parts[0]),
        part_shapes[:1], name="heavy_rows",
    )
    (state,) = call(
        kept_kernel, (state, mixed, ball_order, w_ball_out, heavy[0]), [grid], name="kept_rows"
    )
    parts = relay(parts, members, False)
    rows_in = ((capacity + (members - 1) * wide, width), BF16)
    *parts, mixed = call(
        bound(owner_kernel, wide=wide, **sizes), (state, inbox, w_rot_qkv, *heavy, *parts),
        part_shapes[1:] + [grid16], scratch=[rows_in], name="owner_layer",
    )
    (state,) = call(
        bound(stayed_kernel, **sizes),
        (
            state, mixed, inbox, relay_peer, relay_rank, w_mlp_in, w_mlp_out, w_rot_out, parts[0],
        ),
        [grid], name="stayed_changes",
    )
    parts = relay(parts, members, True)
    rows_in = (((members - 1) * wide, width), BF16)
    (out,) = call(
        bound(last_kernel, wide=wide, **sizes), (state, relay_peer, relay_rank, w_rot_out, *parts),
        [grid], far_outs=(0,), scratch=[rows_in, grid], sems=4, name="relayed_changes",
    )
    return out


def solution(mesh):
    table = P("grp", "rot", None)
    in_specs = (
        P(("grp", "rot"), None), P(), P(),
        P("grp", "rot", None, None, None, None),
        P("grp", "rot", None, None), P("grp", "rot", None, None),
        P("grp", "rot", None, None, None),
        P("grp", "rot", None, None), table, table,
        P(), P(), P(), P(), P(), P(),
        table, table, P("grp", "rot", None, None),
    )
    out_specs = P(("grp", "rot"), None)
    return jax.shard_map(local, mesh=mesh, in_specs=in_specs, out_specs=out_specs, check_vma=False)
```

```python
import math

import jax
import jax.numpy as jnp
from jax import lax
from jax.experimental import pallas as pl
from jax.experimental.pallas import tpu as pltpu
from jax.sharding import PartitionSpec as P

HEADS = 8
BALL = 256
EPSILON = 1e-06
F32 = jnp.float32
BF16 = jnp.bfloat16
LANES = 128
DIGIT = 32


def up_to(count, unit):
    return -(-count // unit) * unit


def dot(left, right):
    return jnp.dot(left, right, preferred_element_type=F32)


def dot_rows(left, right):
    return lax.dot_general(left, right, (((1,), (1,)), ((), ())), preferred_element_type=F32)


def normed(values):
    return values * lax.rsqrt(jnp.mean(values * values, axis=-1, keepdims=True) + EPSILON)


def iota(shape, axis):
    return lax.broadcasted_iota(jnp.int32, shape, axis)


def hot(mask):
    return jnp.where(mask, 1.0, 0.0).astype(BF16)


def column(lane_row):
    return jnp.transpose(jnp.broadcast_to(lane_row, (LANES, LANES)))


def columns(lane_rows):
    count = lane_rows.shape[1]
    return jnp.concatenate([column(lane_rows[:, at : at + LANES]) for at in range(0, count, LANES)], axis=0)


def picks_by(cols, width):
    lane = iota(cols.shape, 1)
    return jnp.concatenate([hot(cols == lane + at) for at in range(0, width, LANES)], axis=1)


def picks(lane_rows, width):
    return picks_by(columns(lane_rows), width)


def places(lane_rows, height):
    return hot(iota((height, lane_rows.shape[1]), 0) == lane_rows)


def attention(rows_in, weight_qkv, store, late=False):
    width = rows_in.shape[1]
    head = width // HEADS
    scale = math.log2(math.e) / math.sqrt(head)
    lane_head = iota((1, width), 1) // head
    masks = [hot(lane_head == h) for h in range(HEADS)]
    joined = dot(rows_in, weight_qkv).astype(BF16)

    def mix(ball, weights, scales, values):
        spread = jnp.concatenate([values * mask for mask in masks], axis=0)
        mixed = dot(jnp.concatenate(weights, axis=1), spread)
        if late:
            scale_of = jnp.broadcast_to(scales[0], mixed.shape)
            for h in range(1, HEADS):
                scale_of = jnp.where(lane_head == h, scales[h], scale_of)
            mixed = mixed * scale_of
        store(ball, mixed.astype(BF16))

    pending = None
    for ball in range(rows_in.shape[0] // BALL):
        own = joined[ball * BALL : (ball + 1) * BALL]
        query, keys, values = own[:, :width], own[:, width : 2 * width], own[:, 2 * width :]
        weights, scales = [], []
        for h in range(HEADS):
            near = slice(h * head // LANES * LANES, (h * head // LANES + 1) * LANES)
            scores = dot_rows(query[:, near] * masks[h][:, near], keys[:, near])
            top = jnp.max(scores, axis=-1, keepdims=True)
            raw = jnp.exp2((scores - top) * scale)
            scales.append(1.0 / jnp.sum(raw, axis=-1, keepdims=True))
            weights.append((raw if late else raw * scales[-1]).astype(BF16))
        if pending is not None:
            mix(*pending)
        pending = (ball, weights, scales, values)
    mix(*pending)


def gelu(values):
    root = math.sqrt(2.0 / math.pi)
    inner = values * (root + (root * 0.044715) * (values * values))
    return values * (0.5 + 0.5 * jnp.tanh(inner))


def rim_kernel(rim_rows, chosen):
    par_grp, par_rot = lax.rem(lax.axis_index("grp"), 2), lax.rem(lax.axis_index("rot"), 2)
    for at, side in enumerate((1 - par_grp, par_grp, 3 - par_rot, 2 + par_rot)):
        chosen[at] = columns(rim_rows[0, 0, pl.ds(side, 1), :])


def make_rims(messages, chosen, out_refs):
    for at, out in enumerate(out_refs):
        out[: chosen.shape[1], :] = dot(picks_by(chosen[at], messages.shape[0]), messages).astype(BF16)


def first_kernel(chosen, features, w_msg, inbox, messages_out, *rims_out):
    points, width = features.shape
    messages = [
        dot(normed(features[at : at + BALL, :].astype(F32)).astype(BF16), w_msg[0]).astype(BF16)
        for at in range(0, points, BALL)
    ]
    messages = jnp.concatenate(messages, axis=0)
    messages_out[...] = messages
    make_rims(messages, chosen, rims_out)
    table = inbox[0, 0]
    pieces = [table[:, at : at + width] for at in range(0, table.shape[1], width)]
    digits = [piece // DIGIT for piece in pieces] + [lax.rem(piece, DIGIT) for piece in pieces]
    digits = jnp.concatenate(digits, axis=0).astype(F32).astype(BF16)
    for out in rims_out:
        out[chosen.shape[1] :, :] = digits


def slots_kernel(
    order, peer, rank, rec2, rec3, after, slots_out, inbox_out, *, members, capacity, light, rim
):
    me = lax.axis_index("rot")
    slots = slot_of(peer[0], rank[0], me, members, capacity, light)
    points = slots.shape[1]
    digits = jnp.concatenate([slots // LANES, lax.rem(slots, LANES)] + [jnp.zeros_like(slots)] * 6, axis=0)
    moved = dot(digits.astype(F32).astype(BF16), places(order[0], points)).astype(jnp.int32)
    slots_out[0:1, :] = slots
    slots_out[1:2, :] = moved[0:1] * LANES + moved[1:2]
    even = (lax.rem(me, 2) == 0).astype(F32)
    table = rec2[rim:, :].astype(F32) * even + rec3[rim:, :].astype(F32) * (1.0 - even)
    half = table.shape[0] // 2
    table = (table[:half] * DIGIT + table[half:]).astype(jnp.int32)
    width = table.shape[1]
    for at in range(0, capacity, width):
        first = at // width * members
        inbox_out[:, at : at + width] = table[first : first + members]


def local_kernel(messages, tiles, source, live, aggregate):
    tile = tiles.shape[-1]
    blocks, sources = tiles.shape[2], tiles.shape[3]
    for b in range(blocks):
        total = None
        for k in range(sources):
            rows = messages[pl.ds(pl.multiple_of(source[0, 0, b, k] * tile, tile), tile), :]
            weight = tiles[0, 0, b, k] * live[0, 0, b, k].astype(BF16)
            part = dot(weight, rows)
            total = part if total is None else total + part
        aggregate[b * tile : (b + 1) * tile, :] = total


def add_border(total, received, tiles, block):
    grp, rot = lax.axis_index("grp"), lax.axis_index("rot")
    par_grp, par_rot = lax.rem(grp, 2), lax.rem(rot, 2)
    sides = (1 - par_grp, par_grp, 3 - par_rot, 2 + par_rot)
    size = tiles.shape[-2]
    for side, rows in zip(sides, received):
        index = jnp.where(side < 2, grp, rot)
        count = jnp.where(side < 2, lax.axis_size("grp"), lax.axis_size("rot"))
        above = lax.rem(side, 2) == 1
        inside = jnp.where(above, index + 1 < count, index > 0)
        part = dot(tiles[0, 0, pl.ds(side, 1)][0], rows[: tiles.shape[-1], :]) * inside.astype(F32)
        at = pl.ds(pl.multiple_of(block[0, 0, side] * size, size), size)
        total[at, :] += part


def middle_kernel(
    state, aggregate, rec0, rec1, rec2, rec3, tiles, block, w_msg, w_upd, chosen,
    state_out, messages_out, rim0, rim1, rim2, rim3, total,
):
    total[...] = aggregate[...]
    add_border(total, (rec0, rec1, rec2, rec3), tiles, block)
    new = state[...].astype(F32) + dot(gelu(total[...]).astype(BF16), w_upd[0])
    state_out[...] = new
    messages = dot(normed(new).astype(BF16), w_msg[1]).astype(BF16)
    messages_out[...] = messages
    make_rims(messages, chosen, (rim0, rim1, rim2, rim3))


def partner(me, step, members):
    return me ^ step if members & (members - 1) == 0 else (me + step) % members


def slot_of(peer, rank, me, members, capacity, light):
    worker = lax.rem(peer - 1 + members, members)
    away = me ^ worker if members & (members - 1) == 0 else lax.rem(worker - me + members, members)
    return jnp.where(away == 0, 0, capacity + light * (away - 1)) + rank


def ball_kernel(
    state, aggregate, rec0, rec1, rec2, rec3, tiles, block, w_upd, order, w_qkv,
    state_out, mixed, total,
):
    total[...] = aggregate[...]
    add_border(total, (rec0, rec1, rec2, rec3), tiles, block)
    points = state.shape[0]
    new = state[...] + dot(gelu(total[...]).astype(BF16), w_upd[1])
    state_out[...] = new
    unit = normed(new).astype(BF16)
    balled = [
        dot(picks(order[0][:, at : at + BALL], points), unit).astype(BF16)
        for at in range(0, points, BALL)
    ]

    def store(ball, value):
        mixed[ball * BALL : (ball + 1) * BALL, :] = value

    attention(jnp.concatenate(balled, axis=0), w_qkv[...], store, late=True)


def feed(pieces, w_in, w_mlp_out):
    inner = [dot(normed(piece).astype(BF16), w_in[...]) for piece in pieces]
    return [
        piece + dot(gelu(values).astype(BF16), w_mlp_out[...])
        for piece, values in zip(pieces, inner)
    ]


def sent_kernel(state, mixed, slots, w_out, w_in, w_mlp_out, *refs, start, after):
    outgoing = refs[after:]
    count = sum(out.shape[0] for out in outgoing)
    at_row = hot(iota((count, slots.shape[1]), 0) + start == slots[0:1, :])
    at_ball = hot(iota((count, slots.shape[1]), 0) + start == slots[1:2, :])
    back = dot(at_ball, mixed[...]).astype(BF16)
    rows = dot(at_row, state[...].astype(BF16))
    step = up_to(count // 3, 16)
    cuts = [slice(at, min(at + step, count)) for at in range(0, count, step)]
    done = feed([rows[cut] + dot(back[cut], w_out[...]) for cut in cuts], w_in, w_mlp_out)
    units = jnp.concatenate([normed(piece).astype(BF16) for piece in done], axis=0)
    at = 0
    for out in outgoing:
        out[...] = units[at : at + out.shape[0]]
        at += out.shape[0]


def kept_kernel(state, mixed, order, w_out, after, state_out):
    back = dot(places(order[0], state.shape[0]), mixed[...]).astype(BF16)
    state_out[...] = state[...] + dot(back, w_out[...])


def owner_kernel(after, inbox, w_qkv, *refs, members, capacity, light, wide):
    incoming, returned = refs[:members], refs[members : 2 * members - 1]
    mixed, rows_in = refs[2 * members - 1 :]
    me = lax.axis_index("rot")
    points = mixed.shape[0]
    indices = []
    at = 0
    for away, rows in enumerate(incoming):
        height = rows.shape[0]
        span = capacity if away == 0 else wide
        sender = partner(me, away if members & (members - 1) == 0 else members - away, members)
        rows_in[at : at + height, :] = rows[...]
        if span > height:
            rows_in[at + height : at + span, :] = jnp.zeros((span - height, rows_in.shape[1]), BF16)
        indices.append(inbox[pl.ds(sender, 1), :][:, :span])
        at += span
    index_row = jnp.concatenate(indices, axis=1)
    owned = dot(places(index_row, points), rows_in[...]).astype(BF16)

    def store(ball, value):
        mixed[ball * BALL : (ball + 1) * BALL, :] = value

    attention(owned, w_qkv[...], store)
    chosen = jnp.concatenate([picks(index, points)[:light] for index in indices[1:]], axis=0)
    back = dot(chosen, mixed[...]).astype(BF16)
    for at, out in enumerate(returned):
        out[...] = back[at * light : (at + 1) * light]


def stayed_kernel(
    state, mixed, inbox, peer, rank, w_in, w_mlp_out, w_out, after, out,
    *, members, capacity, light,
):
    me = lax.axis_index("rot")
    back = dot(picks(inbox[pl.ds(me, 1), :], mixed.shape[0]), mixed[...]).astype(BF16)
    slots = slot_of(peer[0], rank[0], me, members, capacity, light)
    update = dot(picks(slots, capacity), back).astype(BF16)
    starts = range(0, state.shape[0], BALL)
    pieces = feed([state[at : at + BALL, :] for at in starts], w_in, w_mlp_out)
    for at, piece in zip(starts, pieces):
        out[at : at + BALL, :] = piece + dot(update[at : at + BALL], w_out[...])


def last_kernel(state, peer, rank, w_out, *refs, members, capacity, light, wide):
    returned, out, rows_in, new, sems = refs[: members - 1], *refs[members - 1 :]
    me = lax.axis_index("rot")
    for at, rows in enumerate(returned):
        rows_in[at * wide : at * wide + light, :] = rows[...]
        if wide > light:
            rows_in[at * wide + light : (at + 1) * wide, :] = jnp.zeros(
                (wide - light, rows_in.shape[1]), BF16
            )
    slots = slot_of(peer[0], rank[0], me, members, capacity, wide) - capacity
    change = dot(rows_in[...], w_out[...]).astype(BF16)
    update = dot(picks(slots, rows_in.shape[0]), change)
    step = state.shape[0] // 4
    copies = []
    for c in range(4):
        rows = slice(c * step, (c + 1) * step)
        new[rows, :] = state[rows, :] + update[rows]
        copies.append(pltpu.make_async_copy(new.at[rows], out.at[rows], sems.at[c]))
        copies[-1].start()
    for copy in copies:
        copy.wait()


VMEM = pl.BlockSpec(memory_space=pltpu.VMEM)
SMEM = pl.BlockSpec(memory_space=pltpu.SMEM)


def call(kernel, args, outs, scalars=(), far_outs=(), scratch=(), sems=0, flops=0, moved=1 << 20, name=None):
    return pl.pallas_call(
        kernel,
        out_shape=[jax.ShapeDtypeStruct(shape, kind) for shape, kind in outs],
        in_specs=[SMEM if i in scalars else VMEM for i in range(len(args))],
        out_specs=[pl.BlockSpec(memory_space=pl.ANY) if i in far_outs else VMEM for i in range(len(outs))],
        scratch_shapes=[pltpu.VMEM(shape, kind) for shape, kind in scratch]
        + ([pltpu.SemaphoreType.DMA((sems,))] if sems else []),
        compiler_params=pltpu.CompilerParams(vmem_limit_bytes=48 * 1024 * 1024),
        cost_estimate=pl.CostEstimate(flops=flops, bytes_accessed=moved, transcendentals=0),
        name=name,
    )(*args)


def bound(kernel, **kw):
    return lambda *refs: kernel(*refs, **kw)


def swaps(axis, first):
    n_grp, n_rot = lax.axis_size("grp"), lax.axis_size("rot")
    count = n_grp if axis == "grp" else n_rot
    partner = {i: i for i in range(count)}
    for low in range(first, count - 1, 2):
        partner[low], partner[low + 1] = low + 1, low
    if axis == "rot" and first == 1 and count % 2 == 0:
        partner[0], partner[count - 1] = count - 1, 0
    out = []
    for g in range(n_grp):
        for r in range(n_rot):
            to = (partner[g], r) if axis == "grp" else (g, partner[r])
            if to == (g, r) and axis == "grp" and n_rot % 2 == 0:
                to = (g, r ^ 1)
            out.append((g * n_rot + r, to[0] * n_rot + to[1]))
    return out


def exchange(rims):
    plan = [swaps("grp", 0), swaps("grp", 1), swaps("rot", 0), swaps("rot", 1)]
    moved = [None] * 4
    for i in (1, 0, 3, 2):
        moved[i] = lax.ppermute(rims[i], ("grp", "rot"), plan[i])
    return moved


def relay(parts, members, back):
    moved = []
    for at, rows in enumerate(parts):
        pairs = [(i, int(partner(i, at + 1, members))) for i in range(members)]
        moved.append(lax.ppermute(rows, "rot", [pair[::-1] for pair in pairs] if back else pairs))
    return moved


def local(
    features, w_msg, w_upd, local_tiles, local_src, local_live, border_tiles, border_rows,
    border_block, ball_order, w_ball_qkv, w_ball_out, w_mlp_in, w_mlp_out, w_rot_qkv,
    w_rot_out, relay_peer, relay_rank, relay_inbox,
):
    points, width = features.shape
    members, capacity = lax.axis_size("rot"), relay_inbox.shape[-1]
    rim = border_rows.shape[-1]
    most = up_to(points - capacity, members - 1) // (members - 1)
    light, wide = up_to(most, 16), up_to(most, LANES)
    digits = 2 * members * (capacity // width)
    rims_shape = [((rim, width), BF16)] * 4
    first_shape = [((rim + digits, width), BF16)] * 4
    grid, grid16 = ((points, width), F32), ((points, width), BF16)

    (chosen,) = call(
        rim_kernel, (border_rows,), [((4, rim, LANES), jnp.int32)], flops=1 << 31,
        moved=1 << 23, name="rim_rows",
    )
    sizes = dict(members=members, capacity=capacity, light=light)
    part_shapes = [((capacity, width), BF16)] + [((light, width), BF16)] * (members - 1)

    messages, *rims = call(
        first_kernel, (chosen, features, w_msg, relay_inbox), [grid16] + first_shape,
        name="first_messages",
    )
    received = exchange(rims)
    (aggregate,) = call(
        local_kernel, (messages, local_tiles, local_src, local_live), [grid], scalars=(2, 3),
        name="local_edges",
    )
    state, messages, *rims = call(
        middle_kernel,
        (features, aggregate, *received, border_tiles, border_block, w_msg, w_upd, chosen),
        [grid, grid16] + rims_shape, scalars=(7,), scratch=[grid], name="second_messages",
    )
    slots, inbox = call(
        bound(slots_kernel, rim=rim, **sizes),
        (ball_order, relay_peer, relay_rank, received[2], received[3], messages),
        [((2, points), jnp.int32), ((members, capacity), jnp.int32)], name="slots",
    )
    received = exchange(rims)
    (aggregate,) = call(
        local_kernel, (messages, local_tiles, local_src, local_live), [grid], scalars=(2, 3),
        name="local_edges_again",
    )
    state, mixed = call(
        ball_kernel,
        (
            state, aggregate, *received, border_tiles, border_block, w_upd, ball_order,
            w_ball_qkv,
        ),
        [grid, grid16], scalars=(7,), scratch=[grid], name="ball_attention",
    )
    weights = (w_ball_out, w_mlp_in, w_mlp_out)
    parts = call(
        bound(sent_kernel, start=capacity, after=0), (state, mixed, slots, *weights),
        part_shapes[1:], name="light_rows",
    )
    heavy = call(
        bound(sent_kernel, start=0, after=1), (state, mixed, slots, *weights, parts[0]),
        part_shapes[:1], name="heavy_rows",
    )
    (state,) = call(
        kept_kernel, (state, mixed, ball_order, w_ball_out, heavy[0]), [grid], name="kept_rows"
    )
    parts = relay(parts, members, False)
    rows_in = ((capacity + (members - 1) * wide, width), BF16)
    *parts, mixed = call(
        bound(owner_kernel, wide=wide, **sizes), (state, inbox, w_rot_qkv, *heavy, *parts),
        part_shapes[1:] + [grid16], scratch=[rows_in], name="owner_layer",
    )
    (state,) = call(
        bound(stayed_kernel, **sizes),
        (
            state, mixed, inbox, relay_peer, relay_rank, w_mlp_in, w_mlp_out, w_rot_out, parts[0],
        ),
        [grid], name="stayed_changes",
    )
    parts = relay(parts, members, True)
    rows_in = (((members - 1) * wide, width), BF16)
    (out,) = call(
        bound(last_kernel, wide=wide, **sizes), (state, relay_peer, relay_rank, w_rot_out, *parts),
        [grid], far_outs=(0,), scratch=[rows_in, grid], sems=4, name="relayed_changes",
    )
    return out


def solution(mesh):
    table = P("grp", "rot", None)
    in_specs = (
        P(("grp", "rot"), None), P(), P(),
        P("grp", "rot", None, None, None, None),
        P("grp", "rot", None, None), P("grp", "rot", None, None),
        P("grp", "rot", None, None, None),
        P("grp", "rot", None, None), table, table,
        P(), P(), P(), P(), P(), P(),
        table, table, P("grp", "rot", None, None),
    )
    out_specs = P(("grp", "rot"), None)
    return jax.shard_map(local, mesh=mesh, in_specs=in_specs, out_specs=out_specs, check_vma=False)
```
